32 devices in a mesh: pulse: 8 (over y, x, core), range: 4 (over z).
Axes of the slice: x: 2, y: 2, z: 4, core: 2. Of those that a mesh axis runs over, the one named last changes fastest.
Arguments:
- raw_echoes: bfloat16 [512, 4096], P(('pulse', 'range')), may hold values from -6 to 6
- range_taps: bfloat16 [2048, 2], replicated, may hold values from -0.09375 to 0.09375
- mig_offset: int32 [2048], replicated, may hold values from -56 to 56
- interp_band: int32 [2048], replicated, may hold values from 0 to 15
- interp_table: bfloat16 [16, 8], replicated, may hold values from -2 to 2
- azimuth_taps: bfloat16 [1024, 2], replicated, may hold values from -0.125 to 0.125
- geo_list: int32 [32, 8, 4], P(('pulse', 'range')), may hold values from 0 to 255, as said below
- geo_frac: float32 [32, 8, 4], P(('pulse', 'range')), may hold values from 0.1 to 1
Outputs:
- focused: bfloat16 [512, 4096], P(None, ('pulse', 'range'))
- geo_tiles: float32 [256, 1024], P(('pulse', 'range'))
The draws below stay inside these ranges and needn't reach their ends.
Inputs may be any that keep to these rules, and one draw needn't show every extreme that they name: `geo_list`: each entry names a map tile of the patch's own range strip or of one of the two strips beside it; tile t belongs to strip t // 8.
All inputs are finite; a program needn't handle non-finite values.
Results may differ from the reference program's by a relative error of at most 0.005.
The reference program's roundings to bfloat16 on the way count: a program that leaves them out, or rounds other values in their place, can miss the bound.
Values may be sent and summed in bfloat16 or wider, within the bound.
A program may use at most 128 MiB of HBM per device.

```python
import math
import jax
import jax.numpy as jnp
from jax import lax

RTAPS = 2048
ATAPS = 1024
MTAPS = 8
NBANDS = 16
MAXOFF = 56
LOOKS = 4
PROWS = 16
OVL = 4
PUL_DEV = 16
RBIN_DEV = 64
NSTRIP = 32
NP = 512
RB = 2048
NQ = 128
NPATCH = 8


def draw_mig_offset(key, part):
    first, second, third = jax.random.split(key, 3)
    values = jax.random.randint(first, (RB,), -MAXOFF, MAXOFF + 1, dtype=jnp.int32)
    highest = jax.random.randint(second, (), 0, RB, dtype=jnp.int32)
    stride = jax.random.randint(third, (), 1, RB, dtype=jnp.int32)
    lowest = (highest + stride) % RB
    values = values.at[highest].set(MAXOFF)
    values = values.at[lowest].set(-MAXOFF)
    return values.astype(jnp.int32)


def draw_geo_list(key, part):
    first, second = jax.random.split(key, 2)
    shape = (NSTRIP, NPATCH, OVL)
    delta = jax.random.randint(first, shape, -1, 2, dtype=jnp.int32)
    strips = jnp.arange(NSTRIP, dtype=jnp.int32)[:, None, None]
    target = jnp.clip(strips + delta, 0, NSTRIP - 1)
    slots = jax.random.randint(second, shape, 0, NPATCH, dtype=jnp.int32)
    tiles = target * NPATCH + slots
    tiles = tiles.at[0, 0, 0].set(0)
    tiles = tiles.at[NSTRIP - 1, NPATCH - 1, OVL - 1].set(NSTRIP * NPATCH - 1)
    return tiles.astype(jnp.int32)


def set_ends(array, key, least, top_value):
    extent = array.shape
    spot = [jax.random.randint(jax.random.fold_in(key, axis), (), 0, extent[axis]) for axis in range(len(extent))]
    array = array.at[tuple(spot)].set(least)
    longest = extent.index(max(extent))
    spot[longest] = (spot[longest] + 1) % extent[longest]
    return array.at[tuple(spot)].set(top_value)


def level_of(rng, extent, shards, low, top_value):
    def one(axis_at, parts):
        steps = jax.random.uniform(jax.random.fold_in(jax.random.fold_in(rng, 6), axis_at), (parts,), jnp.float32, low / len(shards), top_value / len(shards))
        return jnp.repeat(jnp.exp(steps), extent[axis_at] // parts).reshape((-1,) + (1,) * (len(extent) - axis_at - 1))

    level = one(*shards[0])
    for cut in shards[1:]:
        level = level * one(*cut)
    return level


def noise(key, extent, spread, bound, shards=(), held_as=jnp.bfloat16):
    result = spread * jax.random.normal(key, extent, jnp.float32)
    if shards:
        result = result * level_of(key, extent, shards, -0.22, 0.18)
    return jnp.clip(result, -bound, bound).astype(held_as)


def setup_inputs(seed: int = 0) -> dict:
    streams_of = jax.random.split(jax.random.key(seed), 9)
    return {
        "raw_echoes": noise(streams_of[0], (NP, 2 * RB), 1.0, 6.0, ((0, 32),)),
        "range_taps": noise(streams_of[1], (RTAPS, 2), (2 * RTAPS) ** -0.5, 0.09375),
        "mig_offset": draw_mig_offset(jax.random.fold_in(streams_of[8], 71), 0),
        "interp_band": set_ends(jax.random.randint(streams_of[3], (RB,), 0, NBANDS), jax.random.fold_in(streams_of[3], 1), 0, NBANDS - 1).astype(jnp.int32),
        "interp_table": noise(streams_of[4], (NBANDS, MTAPS), 0.35, 2.0),
        "azimuth_taps": noise(streams_of[5], (ATAPS, 2), (2 * ATAPS) ** -0.5, 0.125),
        "geo_list": draw_geo_list(jax.random.fold_in(streams_of[8], 71), 0),
        "geo_frac": jnp.clip(jnp.exp(math.log(1.0) - 2.3025851 * jax.random.uniform(streams_of[7], (NSTRIP, NPATCH, OVL), jnp.float32) ** level_of(streams_of[7], (NSTRIP, NPATCH, OVL), ((0, 32),), -0.2, 0.2)), 0.1, 1.0),
    }


def toeplitz_block(vector, size):
    flipped = jnp.concatenate([vector[::-1], jnp.zeros((1,), vector.dtype)])
    tiled = jnp.tile(flipped, size)[: size * (2 * size - 1)].reshape(size, 2 * size - 1)
    return tiled[:, size - 1: 2 * size - 1]


def range_matrices(range_taps, dtype):
    block = range_taps.shape[0] // 8
    taps = range_taps.astype(jnp.float32)
    padded = jnp.concatenate([jnp.zeros((block - 1, 2), jnp.float32), taps, jnp.zeros((block, 2), jnp.float32)], 0)
    matrices = []
    for offset in range(9):
        window = padded[offset * block: offset * block + 2 * block - 1]
        real_part = toeplitz_block(window[:, 0], block)
        imag_part = toeplitz_block(window[:, 1], block)
        upper = jnp.stack([real_part, imag_part], -1)
        lower = jnp.stack([-imag_part, real_part], -1)
        matrices.append(jnp.stack([upper, lower], 1).reshape(2 * block, 2 * block).astype(dtype))
    return matrices


def azimuth_matrices(azimuth_taps, dtype):
    block = azimuth_taps.shape[0] // 4
    taps = azimuth_taps.astype(jnp.float32)
    padded = jnp.concatenate([jnp.zeros((block - 1, 2), jnp.float32), taps, jnp.zeros((block, 2), jnp.float32)], 0)
    matrices = []
    for offset in range(5):
        window = padded[offset * block: offset * block + 2 * block - 1]
        joined = jnp.concatenate([toeplitz_block(window[:, 0], block), toeplitz_block(window[:, 1], block)], 1)
        matrices.append(joined.astype(dtype))
    return matrices


def filter_lines(lines, matrices):
    breadth = matrices[0].shape[0]
    line_count = lines.shape[0]
    block_count = lines.shape[1] // breadth
    blocks = lines.reshape(line_count, block_count, breadth)
    padded = jnp.concatenate([blocks, jnp.zeros((line_count, len(matrices) - 1, breadth), lines.dtype)], 1)
    summed = jnp.zeros((line_count * block_count, breadth), jnp.float32)
    for offset, matrix in enumerate(matrices):
        segment = padded[:, offset: offset + block_count].reshape(line_count * block_count, breadth)
        summed = summed + jnp.dot(segment, matrix, preferred_element_type=jnp.float32)
    return summed.reshape(line_count, block_count * breadth)


def compress(columns, matrices):
    block = matrices[0].shape[0]
    length = columns.shape[0]
    breadth = columns.shape[1]
    block_count = length // block
    blocks = columns.reshape(block_count, block, breadth)
    padded = jnp.concatenate([blocks, jnp.zeros((len(matrices) - 1, block, breadth), columns.dtype)], 0)
    summed = jnp.zeros((block_count, 2 * block, breadth), jnp.float32)
    for offset, matrix in enumerate(matrices):
        summed = summed + jnp.einsum("bmr,mn->bnr", padded[offset: offset + block_count], matrix, preferred_element_type=jnp.float32)
    direct = summed[:, :block].reshape(block_count, block, breadth // 2, 2)
    crossed = summed[:, block:].reshape(block_count, block, breadth // 2, 2)
    real_part = direct[..., 0] - crossed[..., 1]
    imag_part = direct[..., 1] + crossed[..., 0]
    return jnp.stack([real_part, imag_part], -1).reshape(length, breadth)


def migrate(lines, offsets, bands, table, margin):
    bin_count = offsets.shape[0]
    band_count = table.shape[0]
    tap_count = table.shape[1]
    selector = (bands[:, None] == jnp.arange(band_count, dtype=jnp.int32)[None, :]).astype(jnp.float32)
    kernels = jnp.dot(selector, table.astype(jnp.float32), precision=lax.Precision.HIGHEST, preferred_element_type=jnp.float32)
    positions = jnp.arange(bin_count, dtype=jnp.int32)
    parity = jnp.arange(2 * bin_count, dtype=jnp.int32) % 2
    summed = jnp.zeros((lines.shape[0], 2 * bin_count), jnp.float32)
    for tap_index in range(tap_count):
        source = positions + offsets + (tap_index - tap_count // 2 + 1 + margin)
        picked = (jnp.repeat(source, 2) * 2 + parity).astype(jnp.int32)
        weights = jnp.repeat(kernels[:, tap_index], 2)
        summed = summed + jnp.take(lines, picked, axis=1).astype(jnp.float32) * weights[None, :]
    return summed


def reference(raw_echoes, range_taps, mig_offset, interp_band, interp_table, azimuth_taps, geo_list, geo_frac):
    margin = MAXOFF + 4
    range_set = range_matrices(range_taps, jnp.float32)

    def range_section(lines):
        filtered = filter_lines(lines.astype(jnp.float32), range_set).astype(jnp.bfloat16)
        padded = jnp.pad(filtered, ((0, 0), (2 * margin, 2 * margin)))
        return migrate(padded, mig_offset, interp_band, interp_table, margin).astype(jnp.bfloat16)

    migrated = lax.map(range_section, raw_echoes.reshape(NSTRIP, PUL_DEV, 2 * RB)).reshape(NP, 2 * RB)
    azimuth_set = azimuth_matrices(azimuth_taps, jnp.float32)

    def azimuth_section(columns):
        focus = compress(columns.astype(jnp.float32), azimuth_set)
        power = focus.reshape(NQ, LOOKS, RBIN_DEV, 2)
        looked = jnp.sum(power * power, axis=(1, 3)) / LOOKS
        return focus.astype(jnp.bfloat16), looked

    strip_columns = migrated.reshape(NP, NSTRIP, 2 * RBIN_DEV).transpose(1, 0, 2)
    focused_strips, looked_strips = lax.map(azimuth_section, strip_columns)
    focused = focused_strips.transpose(1, 0, 2).reshape(NP, 2 * RB)
    patches = looked_strips.reshape(NSTRIP, NPATCH, PROWS * RBIN_DEV)
    weighted = geo_frac[:, :, :, None] * patches[:, :, None, :]
    geo_tiles = jax.ops.segment_sum(weighted.reshape(NSTRIP * NPATCH * OVL, PROWS * RBIN_DEV), geo_list.reshape(NSTRIP * NPATCH * OVL), num_segments=NSTRIP * NPATCH)
    return focused, geo_tiles
```

```python
import functools

import jax
import jax.numpy as jnp
from jax import lax
from jax.experimental import pallas as pl
from jax.experimental.pallas import tpu as pltpu
from jax.sharding import PartitionSpec as P

LOOKS = 4
PROWS = 16
LANES = 128
GROUP = 16
MESH = pl.DeviceIdType.MESH


def iota(shape, dim):
    return lax.broadcasted_iota(jnp.int32, shape, dim)


def shifted_rows(taps, width):
    have = min(width, taps.shape[1])
    line = taps[:, :have].astype(jnp.float32)
    if have < width:
        line = jnp.concatenate([line, jnp.zeros((1, width - have), jnp.float32)], 1)
    eight = jnp.broadcast_to(line, (8, width))
    row = iota((8, width), 0)
    for bit in (1, 2, 4):
        eight = jnp.where((row & bit) != 0, pltpu.roll(eight, bit, 1), eight)
    for step in range(LANES // 16):
        halves = []
        for start in (16 * step, 16 * step + 8):
            moved = eight if start == 0 else pltpu.roll(eight, start, 1)
            keep = iota((8, LANES), 1) >= iota((8, LANES), 0) + start
            first = jnp.where(keep, moved[:, :LANES], 0.0)
            halves.append(jnp.concatenate([first, moved[:, LANES:]], 1))
        yield step, jnp.concatenate(halves, 0)


def kernel(
    devices,
    across,
    raw_ref,
    rtaps_ref,
    offset_ref,
    band_ref,
    table_ref,
    ataps_ref,
    list_ref,
    frac_ref,
    focused_ref,
    tiles_ref,
    zr_ref,
    zi_ref,
    zn_ref,
    za_ref,
    x_ref,
    sum_ref,
    f_ref,
    b_ref,
    send_ref,
    recv_ref,
    power_ref,
    low_ref,
    high_ref,
    from_next_ref,
    from_prev_ref,
    send_sem,
    recv_sem,
    low_send_sem,
    high_send_sem,
    low_recv_sem,
    high_recv_sem,
):
    pulse_at, range_at = lax.axis_index("pulse"), lax.axis_index("range")
    me = pulse_at * across + range_at
    rows, breadth = raw_ref.shape
    chunks = breadth // (2 * LANES)
    groups = chunks // GROUP
    pulses = devices * rows
    patches = list_ref.shape[1]
    rwidth = zr_ref.shape[1]
    awidth = za_ref.shape[1]

    def place(index):
        return (lax.div(index, across), lax.rem(index, across))

    barrier = pltpu.get_barrier_semaphore()

    def greet(distance, carry):
        other = lax.rem(me + distance, devices)
        pl.semaphore_signal(barrier, inc=1, device_id=place(other), device_id_type=MESH)
        return carry

    lax.fori_loop(1, devices, greet, 0)

    def each_group(body):
        if groups == 1:
            body(0)
        else:
            lax.fori_loop(0, groups, lambda g, c: (body(g * GROUP), c)[1], 0)

    side = (2 * LANES, 2 * LANES)
    column = iota(side, 1)
    source = 2 * (LANES - 1 - (column % LANES)) + column // LANES
    parts_apart = (iota(side, 0) == source).astype(jnp.float32).astype(jnp.bfloat16)
    lines = jnp.concatenate(
        [raw_ref[:, 2 * LANES * j : 2 * LANES * (j + 1)] for j in range(chunks)], 0
    )
    x_ref[0 : chunks * rows, :] = jnp.dot(
        lines, parts_apart, preferred_element_type=jnp.float32
    ).astype(jnp.bfloat16)
    spare = x_ref.shape[0] - chunks * rows
    if spare:
        x_ref[chunks * rows :, :] = jnp.zeros((spare, 2 * LANES), jnp.bfloat16)

    for step, real_rows in shifted_rows(rtaps_ref[0:1, :], rwidth):
        zr_ref[16 * step : 16 * step + 16, :] = real_rows.astype(jnp.bfloat16)
    for step, imag_rows in shifted_rows(rtaps_ref[1:2, :], rwidth):
        zi_ref[16 * step : 16 * step + 16, :] = imag_rows.astype(jnp.bfloat16)
        zn_ref[16 * step : 16 * step + 16, :] = (-imag_rows).astype(jnp.bfloat16)

    def range_group(first):
        for apart in range(rwidth // LANES):
            count = GROUP - apart if groups == 1 else GROUP
            if count <= 0:
                continue
            at = slice(LANES * apart, LANES * (apart + 1))
            zr, zi, zn = zr_ref[:, at], zi_ref[:, at], zn_ref[:, at]
            weights = jnp.concatenate(
                [jnp.concatenate([zr, zi], 1), jnp.concatenate([zn, zr], 1)], 0
            )
            start = pl.multiple_of((first + apart) * rows, 16)
            product = jnp.dot(
                x_ref[pl.ds(start, count * rows), :],
                weights,
                preferred_element_type=jnp.float32,
            )
            if apart == 0:
                sum_ref[...] = product
            else:
                sum_ref[0 : count * rows, :] += product
        start = pl.multiple_of((first + 1) * rows, 16)
        f_ref[pl.ds(start, GROUP * rows), :] = sum_ref[...].astype(jnp.bfloat16)

    f_ref[0:rows, :] = jnp.zeros((rows, 2 * LANES), jnp.bfloat16)
    f_ref[(chunks + 1) * rows :, :] = jnp.zeros((rows, 2 * LANES), jnp.bfloat16)
    each_group(range_group)

    window = (2 * LANES, LANES)
    lane = iota(window, 0) % LANES
    shift = jnp.where(lane < LANES // 2, -LANES, LANES)
    bin_of = LANES - 1 - lane + jnp.where(iota(window, 0) < LANES, 0, shift)
    delta = bin_of - iota(window, 1) + 3
    taps = table_ref.shape[0]
    bands = table_ref.shape[1]
    table = table_ref[...]
    left = iota((rows, LANES), 1) < LANES // 2

    def migrate_group(first):
        for j in range(GROUP):
            at = pl.multiple_of((first + j) * LANES, LANES)
            offsets = offset_ref[:, pl.ds(at, LANES)]
            chosen = band_ref[:, pl.ds(at, LANES)]
            onehot = (iota((bands, LANES), 0) == chosen).astype(jnp.float32).astype(jnp.bfloat16)
            weights = jnp.dot(table, onehot, preferred_element_type=jnp.float32)
            banded = jnp.zeros(window, jnp.float32)
            for tap in range(taps):
                banded = jnp.where(delta == offsets + tap, weights[tap : tap + 1, :], banded)
            b_ref[j] = banded.astype(jnp.bfloat16)
        for j in range(GROUP):
            start = pl.multiple_of((first + j) * rows, 16)
            before = f_ref[pl.ds(start, rows), :]
            here = f_ref[pl.ds(pl.multiple_of(start + rows, 16), rows), :]
            after = f_ref[pl.ds(pl.multiple_of(start + 2 * rows, 16), rows), :]
            both = []
            for part in (slice(0, LANES), slice(LANES, 2 * LANES)):
                around = jnp.where(left, before[:, part], after[:, part])
                both.append(jnp.concatenate([here[:, part], around], 1))
            moved = jnp.dot(
                jnp.concatenate(both, 0), b_ref[j], preferred_element_type=jnp.float32
            )
            real_part, imag_part = moved[:rows], moved[rows:]
            even = jnp.where(left, real_part, pltpu.roll(imag_part, LANES // 2, 1))
            odd = jnp.where(left, pltpu.roll(real_part, LANES // 2, 1), imag_part)
            send_ref[2 * (first + j)] = even.astype(jnp.bfloat16)
            send_ref[2 * (first + j) + 1] = odd.astype(jnp.bfloat16)

    each_group(migrate_group)

    pl.semaphore_wait(barrier, devices - 1)

    def send(distance, carry):
        other = lax.rem(me + distance, devices)
        pltpu.make_async_remote_copy(
            src_ref=send_ref.at[other],
            dst_ref=recv_ref.at[me],
            send_sem=send_sem,
            recv_sem=recv_sem,
            device_id=place(other),
            device_id_type=MESH,
        ).start()
        return carry

    lax.fori_loop(1, devices, send, 0)
    recv_ref[me] = send_ref[me]

    for step, real_rows in shifted_rows(ataps_ref[0:1, :], awidth):
        za_ref[16 * step : 16 * step + 16, :] = real_rows.astype(jnp.bfloat16)
    for step, imag_rows in shifted_rows(ataps_ref[1:2, :], awidth):
        za_ref[LANES + 16 * step : LANES + 16 * step + 16, :] = imag_rows.astype(jnp.bfloat16)

    base = (me - 1) * patches
    slot = iota((3 * patches, patches), 0) + base
    spread = jnp.zeros((3 * patches, patches), jnp.float32)
    for over in range(list_ref.shape[0]):
        spread += jnp.where(
            list_ref[over : over + 1, :] == slot, frac_ref[over : over + 1, :], 0.0
        )

    square = (LANES, LANES)
    column = iota(square, 1)
    parts_beside = (iota(square, 0) == LANES // 2 * (column % 2) + column // 2)
    parts_beside = parts_beside.astype(jnp.float32).astype(jnp.bfloat16)
    sign = jnp.where(iota(square, 1) < LANES // 2, -1.0, 1.0)

    others = pl.ds(0, devices - 1)
    pltpu.make_async_copy(recv_ref.at[others], recv_ref.at[others], recv_sem).wait()

    for block in range(pulses // LANES):
        depth = min(awidth, pulses - LANES * block)
        first = LANES * block // rows
        columns = recv_ref[first : first + depth // rows].reshape(depth, LANES)
        product = jnp.dot(za_ref[:, :depth], columns, preferred_element_type=jnp.float32)
        focus = product[:LANES] + sign * pltpu.roll(product[LANES:], LANES // 2, 1)
        at = slice(LANES * block, LANES * (block + 1))
        focused_ref[at, :] = jnp.dot(
            focus.astype(jnp.bfloat16), parts_beside, preferred_element_type=jnp.float32
        ).astype(jnp.bfloat16)
        power_ref[at, :] = focus * focus

    stride = LOOKS * PROWS
    left_half = iota((patches, LANES), 1) < LANES // 2
    pieces = []
    for piece in range(stride // (2 * LOOKS)):
        summed = []
        for half in range(2):
            start = 2 * LOOKS * piece + LOOKS * half
            total = power_ref[pl.ds(start, patches, stride=stride), :]
            for look in range(1, LOOKS):
                total += power_ref[pl.ds(start + look, patches, stride=stride), :]
            summed.append(total + pltpu.roll(total, LANES // 2, 1))
        pieces.append(jnp.where(left_half, summed[0], summed[1]) * (1.0 / LOOKS))
    looked = jnp.concatenate(pieces, 1)
    partial = jnp.dot(
        spread, looked, precision=lax.Precision.HIGHEST, preferred_element_type=jnp.float32
    )
    low_ref[...] = partial[:patches]
    high_ref[...] = partial[2 * patches :]

    def low_copy():
        return pltpu.make_async_remote_copy(
            src_ref=low_ref,
            dst_ref=from_next_ref,
            send_sem=low_send_sem,
            recv_sem=low_recv_sem,
            device_id=place(jnp.maximum(me - 1, 0)),
            device_id_type=MESH,
        )

    def high_copy():
        return pltpu.make_async_remote_copy(
            src_ref=high_ref,
            dst_ref=from_prev_ref,
            send_sem=high_send_sem,
            recv_sem=high_recv_sem,
            device_id=place(jnp.minimum(me + 1, devices - 1)),
            device_id_type=MESH,
        )

    @pl.when(me > 0)
    def _():
        low_copy().start()

    @pl.when(me < devices - 1)
    def _():
        high_copy().start()

    tiles_ref[...] = partial[patches : 2 * patches]
    pltpu.make_async_copy(send_ref.at[others], send_ref.at[others], send_sem).wait()

    @pl.when(me < devices - 1)
    def _():
        low_copy().wait_recv()
        tiles_ref[...] += from_next_ref[...]

    @pl.when(me > 0)
    def _():
        high_copy().wait_recv()
        tiles_ref[...] += from_prev_ref[...]

    @pl.when(me > 0)
    def _():
        low_copy().wait_send()

    @pl.when(me < devices - 1)
    def _():
        high_copy().wait_send()


def body(
    raw_echoes, range_taps, mig_offset, interp_band, interp_table, azimuth_taps, geo_list, geo_frac
):
    across = lax.axis_size("range")
    devices = lax.axis_size("pulse") * across
    rows, breadth = raw_echoes.shape
    pulses = rows * devices
    bins = breadth // 2
    chunks = bins // LANES
    patches = geo_list.shape[1]
    tile = PROWS * (bins // devices)
    rwidth = min(bins, range_taps.shape[0] + LANES)
    awidth = min(pulses, azimuth_taps.shape[0] + LANES)
    spare = 0 if chunks == GROUP else rwidth // LANES
    whole = pl.BlockSpec(memory_space=pltpu.VMEM)
    scratch = [
        pltpu.VMEM((LANES, rwidth), jnp.bfloat16),
        pltpu.VMEM((LANES, rwidth), jnp.bfloat16),
        pltpu.VMEM((LANES, rwidth), jnp.bfloat16),
        pltpu.VMEM((2 * LANES, awidth), jnp.bfloat16),
        pltpu.VMEM(((chunks + spare) * rows, 2 * LANES), jnp.bfloat16),
        pltpu.VMEM((GROUP * rows, 2 * LANES), jnp.float32),
        pltpu.VMEM(((chunks + 2) * rows, 2 * LANES), jnp.bfloat16),
        pltpu.VMEM((GROUP, 2 * LANES, LANES), jnp.bfloat16),
        pltpu.VMEM((devices, rows, LANES), jnp.bfloat16),
        pltpu.VMEM((devices, rows, LANES), jnp.bfloat16),
        pltpu.VMEM((pulses, LANES), jnp.float32),
        pltpu.VMEM((patches, tile), jnp.float32),
        pltpu.VMEM((patches, tile), jnp.float32),
        pltpu.VMEM((patches, tile), jnp.float32),
        pltpu.VMEM((patches, tile), jnp.float32),
    ] + [pltpu.SemaphoreType.DMA] * 6
    return pl.pallas_call(
        functools.partial(kernel, devices, across),
        out_shape=(
            jax.ShapeDtypeStruct((pulses, breadth // devices), jnp.bfloat16),
            jax.ShapeDtypeStruct((patches, tile), jnp.float32),
        ),
        in_specs=[whole] * 8,
        out_specs=(whole, whole),
        scratch_shapes=scratch,
        compiler_params=pltpu.CompilerParams(
            collective_id=0, has_side_effects=True, vmem_limit_bytes=40 * 2**20
        ),
    )(
        raw_echoes,
        range_taps.T,
        mig_offset.reshape(1, bins),
        interp_band.reshape(1, bins),
        interp_table.T,
        azimuth_taps.T,
        geo_list[0].T,
        geo_frac[0].T,
    )


def solution(mesh):
    placed = (
        P(("pulse", "range"), None),
        P(),
        P(),
        P(),
        P(),
        P(),
        P(("pulse", "range"), None, None),
        P(("pulse", "range"), None, None),
    )
    return jax.shard_map(
        body,
        mesh=mesh,
        in_specs=placed,
        out_specs=(P(None, ("pulse", "range")), P(("pulse", "range"), None)),
        check_vma=False,
    )
```

```python
import functools

import jax
import jax.numpy as jnp
from jax import lax
from jax.experimental import pallas as pl
from jax.experimental.pallas import tpu as pltpu
from jax.sharding import PartitionSpec as P

LOOKS = 4
PROWS = 16
LANES = 128
GROUP = 16
BATCH = 4
MESH = pl.DeviceIdType.MESH


def iota(shape, dim):
    return lax.broadcasted_iota(jnp.int32, shape, dim)


def shifted_rows(taps, width):
    have = min(width, taps.shape[1])
    line = taps[:, :have].astype(jnp.float32)
    if have < width:
        line = jnp.concatenate([line, jnp.zeros((1, width - have), jnp.float32)], 1)
    eight = jnp.broadcast_to(line, (8, width))
    row = iota((8, width), 0)
    for bit in (1, 2, 4):
        eight = jnp.where((row & bit) != 0, pltpu.roll(eight, bit, 1), eight)
    for step in range(LANES // 16):
        halves = []
        for start in (16 * step, 16 * step + 8):
            moved = eight if start == 0 else pltpu.roll(eight, start, 1)
            keep = iota((8, LANES), 1) >= iota((8, LANES), 0) + start
            first = jnp.where(keep, moved[:, :LANES], 0.0)
            halves.append(jnp.concatenate([first, moved[:, LANES:]], 1))
        yield step, jnp.concatenate(halves, 0)


def kernel(
    devices,
    across,
    raw_in,
    rtaps_in,
    offset_in,
    band_in,
    table_in,
    ataps_in,
    list_in,
    frac_in,
    focused_ref,
    tiles_ref,
    raw_ref,
    rtaps_ref,
    offset_ref,
    band_ref,
    table_ref,
    ataps_ref,
    list_ref,
    frac_ref,
    zr_ref,
    zi_ref,
    zn_ref,
    za_ref,
    x_ref,
    sum_ref,
    f_ref,
    b_ref,
    send_ref,
    recv_ref,
    focus_ref,
    power_ref,
    low_ref,
    high_ref,
    from_next_ref,
    from_prev_ref,
    in_sems,
    send_sem,
    recv_sem,
    low_send_sem,
    high_send_sem,
    low_recv_sem,
    high_recv_sem,
):
    pulse_at, range_at = lax.axis_index("pulse"), lax.axis_index("range")
    me = pulse_at * across + range_at
    rows, breadth = raw_ref.shape
    chunks = breadth // (2 * LANES)
    groups = chunks // GROUP
    pulses = devices * rows
    patches = list_ref.shape[1]
    rwidth = zr_ref.shape[1]
    awidth = za_ref.shape[1]

    rtaps_copy, offset_copy, band_copy, table_copy, raw_copy, ataps_copy, list_copy, frac_copy = [
        pltpu.make_async_copy(outside, inside, in_sems.at[at])
        for at, (outside, inside) in enumerate(
            (
                (rtaps_in, rtaps_ref),
                (offset_in, offset_ref),
                (band_in, band_ref),
                (table_in, table_ref),
                (raw_in, raw_ref),
                (ataps_in, ataps_ref),
                (list_in, list_ref),
                (frac_in, frac_ref),
            )
        )
    ]
    first_copies = (rtaps_copy, offset_copy, band_copy, table_copy, raw_copy)
    later_copies = (ataps_copy, list_copy, frac_copy)
    for copy in first_copies + later_copies:
        copy.start()

    def place(index):
        return (lax.div(index, across), lax.rem(index, across))

    barrier = pltpu.get_barrier_semaphore()

    def greet(distance, carry):
        other = lax.rem(me + distance, devices)
        pl.semaphore_signal(barrier, inc=1, device_id=place(other), device_id_type=MESH)
        return carry

    lax.fori_loop(1, devices, greet, 0)

    def each_group(body):
        if groups == 1:
            body(0)
        else:
            lax.fori_loop(0, groups, lambda g, c: (body(g * GROUP), c)[1], 0)

    for copy in first_copies:
        copy.wait()

    for step, real_rows in shifted_rows(rtaps_ref[0:1, :], rwidth):
        zr_ref[16 * step : 16 * step + 16, :] = real_rows.astype(jnp.bfloat16)
    for step, imag_rows in shifted_rows(rtaps_ref[1:2, :], rwidth):
        zi_ref[16 * step : 16 * step + 16, :] = imag_rows.astype(jnp.bfloat16)
        zn_ref[16 * step : 16 * step + 16, :] = (-imag_rows).astype(jnp.bfloat16)

    side = (2 * LANES, 2 * LANES)
    column = iota(side, 1)
    source = 2 * (LANES - 1 - (column % LANES)) + column // LANES
    parts_apart = (iota(side, 0) == source).astype(jnp.float32).astype(jnp.bfloat16)
    lines = jnp.concatenate(
        [raw_ref[:, 2 * LANES * j : 2 * LANES * (j + 1)] for j in range(chunks)], 0
    )
    x_ref[0 : chunks * rows, :] = jnp.dot(
        lines, parts_apart, preferred_element_type=jnp.float32
    ).astype(jnp.bfloat16)
    spare = x_ref.shape[0] - chunks * rows
    if spare:
        x_ref[chunks * rows :, :] = jnp.zeros((spare, 2 * LANES), jnp.bfloat16)

    def range_group(first):
        for apart in range(rwidth // LANES):
            count = GROUP - apart if groups == 1 else GROUP
            if count <= 0:
                continue
            at = slice(LANES * apart, LANES * (apart + 1))
            zr, zi, zn = zr_ref[:, at], zi_ref[:, at], zn_ref[:, at]
            weights = jnp.concatenate(
                [jnp.concatenate([zr, zi], 1), jnp.concatenate([zn, zr], 1)], 0
            )
            start = pl.multiple_of((first + apart) * rows, 16)
            product = jnp.dot(
                x_ref[pl.ds(start, count * rows), :],
                weights,
                preferred_element_type=jnp.float32,
            )
            if apart == 0:
                sum_ref[...] = product
            else:
                sum_ref[0 : count * rows, :] += product
        start = pl.multiple_of((first + 1) * rows, 16)
        f_ref[pl.ds(start, GROUP * rows), :] = sum_ref[...].astype(jnp.bfloat16)

    f_ref[0:rows, :] = jnp.zeros((rows, 2 * LANES), jnp.bfloat16)
    f_ref[(chunks + 1) * rows :, :] = jnp.zeros((rows, 2 * LANES), jnp.bfloat16)
    each_group(range_group)

    window = (2 * LANES, LANES)
    lane = iota(window, 0) % LANES
    shift = jnp.where(lane < LANES // 2, -LANES, LANES)
    bin_of = LANES - 1 - lane + jnp.where(iota(window, 0) < LANES, 0, shift)
    delta = bin_of - iota(window, 1) + 3
    taps = table_ref.shape[0]
    bands = table_ref.shape[1]
    table = table_ref[...]
    left = iota((rows, LANES), 1) < LANES // 2

    def migrate_group(first):
        chunk_at = [lax.rem(lax.div(me, 2) + first + 1 + j, chunks) for j in range(GROUP)]
        for j, chunk in enumerate(chunk_at):
            at = pl.multiple_of(chunk * LANES, LANES)
            offsets = offset_ref[:, pl.ds(at, LANES)]
            chosen = band_ref[:, pl.ds(at, LANES)]
            onehot = (iota((bands, LANES), 0) == chosen).astype(jnp.float32).astype(jnp.bfloat16)
            weights = jnp.dot(table, onehot, preferred_element_type=jnp.float32)
            banded = jnp.zeros(window, jnp.float32)
            for tap in range(taps):
                banded = jnp.where(delta == offsets + tap, weights[tap : tap + 1, :], banded)
            b_ref[j] = banded.astype(jnp.bfloat16)

        for j, chunk in enumerate(chunk_at):
            start = pl.multiple_of(chunk * rows, 16)
            before = f_ref[pl.ds(start, rows), :]
            here = f_ref[pl.ds(pl.multiple_of(start + rows, 16), rows), :]
            after = f_ref[pl.ds(pl.multiple_of(start + 2 * rows, 16), rows), :]
            both = []
            for part in (slice(0, LANES), slice(LANES, 2 * LANES)):
                around = jnp.where(left, before[:, part], after[:, part])
                both.append(jnp.concatenate([here[:, part], around], 1))
            moved = jnp.dot(
                jnp.concatenate(both, 0), b_ref[j], preferred_element_type=jnp.float32
            )
            real_part, imag_part = moved[:rows], moved[rows:]
            even = jnp.where(left, real_part, pltpu.roll(imag_part, LANES // 2, 1))
            odd = jnp.where(left, pltpu.roll(real_part, LANES // 2, 1), imag_part)
            send_ref[2 * chunk] = even.astype(jnp.bfloat16)
            send_ref[2 * chunk + 1] = odd.astype(jnp.bfloat16)
            if j % BATCH == BATCH - 1:
                if groups == 1 and j == BATCH - 1:
                    pl.semaphore_wait(barrier, devices - 1)
                for ready in range(j + 1 - BATCH, j + 1):
                    for half in range(2):
                        own_possible = groups > 1 or ready == GROUP - 1
                        send(2 * chunk_at[ready] + half, own_possible)

    def send(other, own_possible):
        def go():
            pltpu.make_async_remote_copy(
                src_ref=send_ref.at[other],
                dst_ref=recv_ref.at[me],
                send_sem=send_sem,
                recv_sem=recv_sem,
                device_id=place(other),
                device_id_type=MESH,
            ).start()

        if own_possible:
            pl.when(other != me)(go)
        else:
            go()

    if groups > 1:
        pl.semaphore_wait(barrier, devices - 1)
    each_group(migrate_group)
    recv_ref[me] = send_ref[me]

    for copy in later_copies:
        copy.wait()
    for step, real_rows in shifted_rows(ataps_ref[0:1, :], awidth):
        za_ref[16 * step : 16 * step + 16, :] = real_rows.astype(jnp.bfloat16)
    for step, imag_rows in shifted_rows(ataps_ref[1:2, :], awidth):
        za_ref[LANES + 16 * step : LANES + 16 * step + 16, :] = imag_rows.astype(jnp.bfloat16)

    base = (me - 1) * patches
    slot = iota((3 * patches, patches), 0) + base
    spread = jnp.zeros((3 * patches, patches), jnp.float32)
    for over in range(list_ref.shape[0]):
        spread += jnp.where(
            list_ref[over : over + 1, :] == slot, frac_ref[over : over + 1, :], 0.0
        )

    square = (LANES, LANES)
    column = iota(square, 1)
    parts_beside = (iota(square, 0) == LANES // 2 * (column % 2) + column // 2)
    parts_beside = parts_beside.astype(jnp.float32).astype(jnp.bfloat16)
    sign = jnp.where(iota(square, 1) < LANES // 2, -1.0, 1.0)

    others = pl.ds(0, devices - 1)
    pltpu.make_async_copy(recv_ref.at[others], recv_ref.at[others], recv_sem).wait()

    for block in range(pulses // LANES):
        depth = min(awidth, pulses - LANES * block)
        first = LANES * block // rows
        columns = recv_ref[first : first + depth // rows].reshape(depth, LANES)
        product = jnp.dot(za_ref[:, :depth], columns, preferred_element_type=jnp.float32)
        focus = product[:LANES] + sign * pltpu.roll(product[LANES:], LANES // 2, 1)
        at = slice(LANES * block, LANES * (block + 1))
        focus_ref[at, :] = focus.astype(jnp.bfloat16)
        power_ref[at, :] = focus * focus

    stride = LOOKS * PROWS
    left_half = iota((patches, LANES), 1) < LANES // 2
    pieces = []
    for piece in range(stride // (2 * LOOKS)):
        summed = []
        for half in range(2):
            start = 2 * LOOKS * piece + LOOKS * half
            total = power_ref[pl.ds(start, patches, stride=stride), :]
            for look in range(1, LOOKS):
                total += power_ref[pl.ds(start + look, patches, stride=stride), :]
            summed.append(total + pltpu.roll(total, LANES // 2, 1))
        pieces.append(jnp.where(left_half, summed[0], summed[1]) * (1.0 / LOOKS))
    looked = jnp.concatenate(pieces, 1)

    def tile_sums(first):
        weights = spread[first : first + patches]
        total = weights[:, 0:1] * looked[0:1, :]
        for patch in range(1, patches):
            total += weights[:, patch : patch + 1] * looked[patch : patch + 1, :]
        return total

    low_ref[...] = tile_sums(0)
    high_ref[...] = tile_sums(2 * patches)

    def low_copy():
        return pltpu.make_async_remote_copy(
            src_ref=low_ref,
            dst_ref=from_next_ref,
            send_sem=low_send_sem,
            recv_sem=low_recv_sem,
            device_id=place(jnp.maximum(me - 1, 0)),
            device_id_type=MESH,
        )

    def high_copy():
        return pltpu.make_async_remote_copy(
            src_ref=high_ref,
            dst_ref=from_prev_ref,
            send_sem=high_send_sem,
            recv_sem=high_recv_sem,
            device_id=place(jnp.minimum(me + 1, devices - 1)),
            device_id_type=MESH,
        )

    @pl.when(me > 0)
    def _():
        low_copy().start()

    @pl.when(me < devices - 1)
    def _():
        high_copy().start()

    tiles_ref[...] = tile_sums(patches)
    focused_ref[...] = jnp.dot(
        focus_ref[...], parts_beside, preferred_element_type=jnp.float32
    ).astype(jnp.bfloat16)
    pltpu.make_async_copy(send_ref.at[others], send_ref.at[others], send_sem).wait()

    @pl.when(me < devices - 1)
    def _():
        low_copy().wait_recv()
        tiles_ref[...] += from_next_ref[...]

    @pl.when(me > 0)
    def _():
        high_copy().wait_recv()
        tiles_ref[...] += from_prev_ref[...]

    @pl.when(me > 0)
    def _():
        low_copy().wait_send()

    @pl.when(me < devices - 1)
    def _():
        high_copy().wait_send()


def hand_out(focused_ref, tiles_ref, focused_out, tiles_out, sems):
    copies = (
        pltpu.make_async_copy(focused_ref, focused_out, sems.at[0]),
        pltpu.make_async_copy(tiles_ref, tiles_out, sems.at[1]),
    )
    for copy in copies:
        copy.start()
    for copy in copies:
        copy.wait()


def body(
    raw_echoes, range_taps, mig_offset, interp_band, interp_table, azimuth_taps, geo_list, geo_frac
):
    across = lax.axis_size("range")
    devices = lax.axis_size("pulse") * across
    rows, breadth = raw_echoes.shape
    pulses = rows * devices
    bins = breadth // 2
    chunks = bins // LANES
    patches = geo_list.shape[1]
    tile = PROWS * (bins // devices)
    rwidth = min(bins, range_taps.shape[0] + LANES)
    awidth = min(pulses, azimuth_taps.shape[0] + LANES)
    spare = 0 if chunks == GROUP else rwidth // LANES
    whole = pl.BlockSpec(memory_space=pltpu.VMEM)
    operands = (
        raw_echoes,
        range_taps.T,
        mig_offset.reshape(1, bins),
        interp_band.reshape(1, bins),
        interp_table.T,
        azimuth_taps.T,
        geo_list[0].T,
        geo_frac[0].T,
    )
    scratch = [pltpu.VMEM(operand.shape, operand.dtype) for operand in operands] + [
        pltpu.VMEM((LANES, rwidth), jnp.bfloat16),
        pltpu.VMEM((LANES, rwidth), jnp.bfloat16),
        pltpu.VMEM((LANES, rwidth), jnp.bfloat16),
        pltpu.VMEM((2 * LANES, awidth), jnp.bfloat16),
        pltpu.VMEM(((chunks + spare) * rows, 2 * LANES), jnp.bfloat16),
        pltpu.VMEM((GROUP * rows, 2 * LANES), jnp.float32),
        pltpu.VMEM(((chunks + 2) * rows, 2 * LANES), jnp.bfloat16),
        pltpu.VMEM((GROUP, 2 * LANES, LANES), jnp.bfloat16),
        pltpu.VMEM((devices, rows, LANES), jnp.bfloat16),
        pltpu.VMEM((devices, rows, LANES), jnp.bfloat16),
        pltpu.VMEM((pulses, LANES), jnp.bfloat16),
        pltpu.VMEM((pulses, LANES), jnp.float32),
        pltpu.VMEM((patches, tile), jnp.float32),
        pltpu.VMEM((patches, tile), jnp.float32),
        pltpu.VMEM((patches, tile), jnp.float32),
        pltpu.VMEM((patches, tile), jnp.float32),
    ] + [pltpu.SemaphoreType.DMA((8,))] + [pltpu.SemaphoreType.DMA] * 6
    shapes = (
        jax.ShapeDtypeStruct((pulses, breadth // devices), jnp.bfloat16),
        jax.ShapeDtypeStruct((patches, tile), jnp.float32),
    )
    outside = pl.BlockSpec(memory_space=pltpu.HBM)
    results = pl.pallas_call(
        functools.partial(kernel, devices, across),
        out_shape=shapes,
        in_specs=[outside] * 8,
        out_specs=(whole, whole),
        scratch_shapes=scratch,
        compiler_params=pltpu.CompilerParams(
            collective_id=0, has_side_effects=True, vmem_limit_bytes=40 * 2**20
        ),
    )(*[pltpu.with_memory_space_constraint(operand, pltpu.HBM) for operand in operands])
    return pl.pallas_call(
        hand_out,
        out_shape=shapes,
        in_specs=[whole] * 2,
        out_specs=(outside, outside),
        scratch_shapes=[pltpu.SemaphoreType.DMA((2,))],
    )(*results)


def solution(mesh):
    placed = (
        P(("pulse", "range"), None),
        P(),
        P(),
        P(),
        P(),
        P(),
        P(("pulse", "range"), None, None),
        P(("pulse", "range"), None, None),
    )
    return jax.shard_map(
        body,
        mesh=mesh,
        in_specs=placed,
        out_specs=(P(None, ("pulse", "range")), P(("pulse", "range"), None)),
        check_vma=False,
    )
```

```python
import functools

import jax
import jax.numpy as jnp
from jax import lax
from jax.experimental import pallas as pl
from jax.experimental.pallas import tpu as pltpu
from jax.sharding import PartitionSpec as P

LOOKS = 4
PROWS = 16
LANES = 128
GROUP = 16
BATCH = 4
MESH = pl.DeviceIdType.MESH


def iota(shape, dim):
    return lax.broadcasted_iota(jnp.int32, shape, dim)


def shifted_rows(taps, width):
    have = min(width, taps.shape[1])
    line = taps[:, :have].astype(jnp.float32)
    if have < width:
        line = jnp.concatenate([line, jnp.zeros((1, width - have), jnp.float32)], 1)
    eight = jnp.broadcast_to(line, (8, width))
    row = iota((8, width), 0)
    for bit in (1, 2, 4):
        eight = jnp.where((row & bit) != 0, pltpu.roll(eight, bit, 1), eight)
    for step in range(LANES // 16):
        halves = []
        for start in (16 * step, 16 * step + 8):
            moved = eight if start == 0 else pltpu.roll(eight, start, 1)
            keep = iota((8, LANES), 1) >= iota((8, LANES), 0) + start
            first = jnp.where(keep, moved[:, :LANES], 0.0)
            halves.append(jnp.concatenate([first, moved[:, LANES:]], 1))
        yield step, jnp.concatenate(halves, 0)


def kernel(
    devices,
    across,
    raw_in,
    rtaps_in,
    offset_in,
    band_in,
    table_in,
    ataps_in,
    list_in,
    frac_in,
    focused_ref,
    tiles_ref,
    raw_ref,
    rtaps_ref,
    offset_ref,
    band_ref,
    table_ref,
    ataps_ref,
    list_ref,
    frac_ref,
    zr_ref,
    zi_ref,
    zn_ref,
    za_ref,
    x_ref,
    sum_ref,
    f_ref,
    kernel_ref,
    b_ref,
    send_ref,
    recv_ref,
    focus_ref,
    power_ref,
    low_ref,
    high_ref,
    from_next_ref,
    from_prev_ref,
    in_sems,
    send_sem,
    recv_sem,
    low_send_sem,
    high_send_sem,
    low_recv_sem,
    high_recv_sem,
):
    pulse_at, range_at = lax.axis_index("pulse"), lax.axis_index("range")
    me = pulse_at * across + range_at
    rows, breadth = raw_ref.shape
    chunks = breadth // (2 * LANES)
    groups = chunks // GROUP
    pulses = devices * rows
    patches = list_ref.shape[1]
    rwidth = zr_ref.shape[1]
    awidth = za_ref.shape[1]

    rtaps_copy, offset_copy, band_copy, table_copy, raw_copy, ataps_copy, list_copy, frac_copy = [
        pltpu.make_async_copy(outside, inside, in_sems.at[at])
        for at, (outside, inside) in enumerate(
            (
                (rtaps_in, rtaps_ref),
                (offset_in, offset_ref),
                (band_in, band_ref),
                (table_in, table_ref),
                (raw_in, raw_ref),
                (ataps_in, ataps_ref),
                (list_in, list_ref),
                (frac_in, frac_ref),
            )
        )
    ]
    first_copies = (rtaps_copy, offset_copy, band_copy, table_copy, raw_copy)
    later_copies = (ataps_copy, list_copy, frac_copy)
    for copy in first_copies + later_copies:
        copy.start()

    def place(index):
        return (lax.div(index, across), lax.rem(index, across))

    barrier = pltpu.get_barrier_semaphore()

    def greet(distance, carry):
        other = lax.rem(me + distance, devices)
        pl.semaphore_signal(barrier, inc=1, device_id=place(other), device_id_type=MESH)
        return carry

    lax.fori_loop(1, devices, greet, 0)

    def each_group(body):
        if groups == 1:
            body(0)
        else:
            lax.fori_loop(0, groups, lambda g, c: (body(g * GROUP), c)[1], 0)

    rtaps_copy.wait()

    for step, real_rows in shifted_rows(rtaps_ref[0:1, :], rwidth):
        zr_ref[16 * step : 16 * step + 16, :] = real_rows.astype(jnp.bfloat16)
    for step, imag_rows in shifted_rows(rtaps_ref[1:2, :], rwidth):
        zi_ref[16 * step : 16 * step + 16, :] = imag_rows.astype(jnp.bfloat16)
        zn_ref[16 * step : 16 * step + 16, :] = (-imag_rows).astype(jnp.bfloat16)

    for copy in first_copies[1:]:
        copy.wait()

    side = (2 * LANES, 2 * LANES)
    column = iota(side, 1)
    source = 2 * (LANES - 1 - (column % LANES)) + column // LANES
    parts_apart = (iota(side, 0) == source).astype(jnp.float32).astype(jnp.bfloat16)
    lines = jnp.concatenate(
        [raw_ref[:, 2 * LANES * j : 2 * LANES * (j + 1)] for j in range(chunks)], 0
    )
    x_ref[0 : chunks * rows, :] = jnp.dot(
        lines, parts_apart, preferred_element_type=jnp.float32
    ).astype(jnp.bfloat16)
    spare = x_ref.shape[0] - chunks * rows
    if spare:
        x_ref[chunks * rows :, :] = jnp.zeros((spare, 2 * LANES), jnp.bfloat16)

    bands, bins = table_ref.shape[1], chunks * LANES
    onehot = (iota((bands, bins), 0) == band_ref[...]).astype(jnp.float32).astype(jnp.bfloat16)
    kernel_ref[...] = jnp.dot(table_ref[...], onehot, preferred_element_type=jnp.float32)
    window = (2 * LANES, LANES)
    lane = iota(window, 0) % LANES
    shift = jnp.where(lane < LANES // 2, -LANES, LANES)
    bin_of = LANES - 1 - lane + jnp.where(iota(window, 0) < LANES, 0, shift)
    delta = (bin_of - iota(window, 1) + 3).astype(jnp.int16)

    def band_matrix(chunk):
        at = pl.ds(pl.multiple_of(chunk * LANES, LANES), LANES)
        offsets = jnp.broadcast_to(offset_ref[:, at], (16, LANES)).astype(jnp.int16)
        distance = delta - jnp.broadcast_to(offsets[0:1], window)
        weights = kernel_ref[:, at]
        banded = jnp.zeros(window, jnp.bfloat16)
        for tap in range(weights.shape[0]):
            weight = jnp.broadcast_to(weights[tap : tap + 1], (16, LANES)).astype(jnp.bfloat16)
            weight = jnp.broadcast_to(weight[0:1], window)
            banded = jnp.where(distance == jnp.int16(tap), weight, banded)
        b_ref[chunk] = banded

    def range_group(first):
        for apart in range(rwidth // LANES):
            count = GROUP - apart if groups == 1 else GROUP
            if apart < GROUP:
                band_matrix(first + apart)
            if count <= 0:
                continue
            at = slice(LANES * apart, LANES * (apart + 1))
            zr, zi, zn = zr_ref[:, at], zi_ref[:, at], zn_ref[:, at]
            weights = jnp.concatenate(
                [jnp.concatenate([zr, zi], 1), jnp.concatenate([zn, zr], 1)], 0
            )
            start = pl.multiple_of((first + apart) * rows, 16)
            product = jnp.dot(
                x_ref[pl.ds(start, count * rows), :],
                weights,
                preferred_element_type=jnp.float32,
            )
            if apart == 0:
                sum_ref[...] = product
            else:
                sum_ref[0 : count * rows, :] += product
        start = pl.multiple_of((first + 1) * rows, 16)
        f_ref[pl.ds(start, GROUP * rows), :] = sum_ref[...].astype(jnp.bfloat16)

    f_ref[0:rows, :] = jnp.zeros((rows, 2 * LANES), jnp.bfloat16)
    f_ref[(chunks + 1) * rows :, :] = jnp.zeros((rows, 2 * LANES), jnp.bfloat16)
    each_group(range_group)

    left = iota((rows, LANES), 1) < LANES // 2

    def migrate_group(first):
        ahead = list(range(1, GROUP, 2)) + list(range(2, GROUP + 1, 2))
        chunk_at = [lax.rem(lax.div(me, 2) + first + step, chunks) for step in ahead]
        for j, chunk in enumerate(chunk_at):
            start = pl.multiple_of(chunk * rows, 16)
            before = f_ref[pl.ds(start, rows), :]
            here = f_ref[pl.ds(pl.multiple_of(start + rows, 16), rows), :]
            after = f_ref[pl.ds(pl.multiple_of(start + 2 * rows, 16), rows), :]
            both = []
            for part in (slice(0, LANES), slice(LANES, 2 * LANES)):
                around = jnp.where(left, before[:, part], after[:, part])
                both.append(jnp.concatenate([here[:, part], around], 1))
            moved = jnp.dot(
                jnp.concatenate(both, 0), b_ref[chunk], preferred_element_type=jnp.float32
            )
            real_part, imag_part = moved[:rows], moved[rows:]
            even = jnp.where(left, real_part, pltpu.roll(imag_part, LANES // 2, 1))
            odd = jnp.where(left, pltpu.roll(real_part, LANES // 2, 1), imag_part)
            send_ref[2 * chunk] = even.astype(jnp.bfloat16)
            send_ref[2 * chunk + 1] = odd.astype(jnp.bfloat16)
            if j % BATCH == BATCH - 1:
                if groups == 1 and j == BATCH - 1:
                    pl.semaphore_wait(barrier, devices - 1)
                for ready in range(j + 1 - BATCH, j + 1):
                    for half in range(2):
                        own_possible = groups > 1 or ready == GROUP - 1
                        send(2 * chunk_at[ready] + half, own_possible)

    def send(other, own_possible):
        def go():
            pltpu.make_async_remote_copy(
                src_ref=send_ref.at[other],
                dst_ref=recv_ref.at[me],
                send_sem=send_sem,
                recv_sem=recv_sem,
                device_id=place(other),
                device_id_type=MESH,
            ).start()

        if own_possible:
            pl.when(other != me)(go)
        else:
            go()

    if groups > 1:
        pl.semaphore_wait(barrier, devices - 1)
    each_group(migrate_group)
    recv_ref[me] = send_ref[me]

    for copy in later_copies:
        copy.wait()
    for step, real_rows in shifted_rows(ataps_ref[0:1, :], awidth):
        za_ref[16 * step : 16 * step + 16, :] = real_rows.astype(jnp.bfloat16)
    for step, imag_rows in shifted_rows(ataps_ref[1:2, :], awidth):
        za_ref[LANES + 16 * step : LANES + 16 * step + 16, :] = imag_rows.astype(jnp.bfloat16)

    base = (me - 1) * patches
    slot = iota((3 * patches, patches), 0) + base
    spread = jnp.zeros((3 * patches, patches), jnp.float32)
    for over in range(list_ref.shape[0]):
        spread += jnp.where(
            list_ref[over : over + 1, :] == slot, frac_ref[over : over + 1, :], 0.0
        )

    square = (LANES, LANES)
    column = iota(square, 1)
    parts_beside = (iota(square, 0) == LANES // 2 * (column % 2) + column // 2)
    parts_beside = parts_beside.astype(jnp.float32).astype(jnp.bfloat16)
    sign = jnp.where(iota(square, 1) < LANES // 2, -1.0, 1.0)

    others = pl.ds(0, devices - 1)
    pltpu.make_async_copy(recv_ref.at[others], recv_ref.at[others], recv_sem).wait()

    for block in range(pulses // LANES):
        depth = min(awidth, pulses - LANES * block)
        first = LANES * block // rows
        columns = recv_ref[first : first + depth // rows].reshape(depth, LANES)
        product = jnp.dot(za_ref[:, :depth], columns, preferred_element_type=jnp.float32)
        focus = product[:LANES] + sign * pltpu.roll(product[LANES:], LANES // 2, 1)
        at = slice(LANES * block, LANES * (block + 1))
        focus_ref[at, :] = focus.astype(jnp.bfloat16)
        power_ref[at, :] = focus * focus

    stride = LOOKS * PROWS
    left_half = iota((patches, LANES), 1) < LANES // 2
    pieces = []
    for piece in range(stride // (2 * LOOKS)):
        summed = []
        for half in range(2):
            start = 2 * LOOKS * piece + LOOKS * half
            total = power_ref[pl.ds(start, patches, stride=stride), :]
            for look in range(1, LOOKS):
                total += power_ref[pl.ds(start + look, patches, stride=stride), :]
            summed.append(total + pltpu.roll(total, LANES // 2, 1))
        pieces.append(jnp.where(left_half, summed[0], summed[1]) * (1.0 / LOOKS))
    looked = jnp.concatenate(pieces, 1)

    def tile_sums(first):
        weights = spread[first : first + patches]
        total = weights[:, 0:1] * looked[0:1, :]
        for patch in range(1, patches):
            total += weights[:, patch : patch + 1] * looked[patch : patch + 1, :]
        return total

    low_ref[...] = tile_sums(0)
    high_ref[...] = tile_sums(2 * patches)

    def low_copy():
        return pltpu.make_async_remote_copy(
            src_ref=low_ref,
            dst_ref=from_next_ref,
            send_sem=low_send_sem,
            recv_sem=low_recv_sem,
            device_id=place(jnp.maximum(me - 1, 0)),
            device_id_type=MESH,
        )

    def high_copy():
        return pltpu.make_async_remote_copy(
            src_ref=high_ref,
            dst_ref=from_prev_ref,
            send_sem=high_send_sem,
            recv_sem=high_recv_sem,
            device_id=place(jnp.minimum(me + 1, devices - 1)),
            device_id_type=MESH,
        )

    @pl.when(me > 0)
    def _():
        low_copy().start()

    @pl.when(me < devices - 1)
    def _():
        high_copy().start()

    tiles_ref[...] = tile_sums(patches)
    focused_ref[...] = jnp.dot(
        focus_ref[...], parts_beside, preferred_element_type=jnp.float32
    ).astype(jnp.bfloat16)
    pltpu.make_async_copy(send_ref.at[others], send_ref.at[others], send_sem).wait()

    @pl.when(me < devices - 1)
    def _():
        low_copy().wait_recv()
        tiles_ref[...] += from_next_ref[...]

    @pl.when(me > 0)
    def _():
        high_copy().wait_recv()
        tiles_ref[...] += from_prev_ref[...]

    @pl.when(me > 0)
    def _():
        low_copy().wait_send()

    @pl.when(me < devices - 1)
    def _():
        high_copy().wait_send()


def body(
    raw_echoes, range_taps, mig_offset, interp_band, interp_table, azimuth_taps, geo_list, geo_frac
):
    across = lax.axis_size("range")
    devices = lax.axis_size("pulse") * across
    rows, breadth = raw_echoes.shape
    pulses = rows * devices
    bins = breadth // 2
    chunks = bins // LANES
    patches = geo_list.shape[1]
    tile = PROWS * (bins // devices)
    rwidth = min(bins, range_taps.shape[0] + LANES)
    awidth = min(pulses, azimuth_taps.shape[0] + LANES)
    spare = 0 if chunks == GROUP else rwidth // LANES
    whole = pl.BlockSpec(memory_space=pltpu.VMEM)
    operands = (
        raw_echoes,
        range_taps.T,
        mig_offset.reshape(1, bins),
        interp_band.reshape(1, bins),
        interp_table.T,
        azimuth_taps.T,
        geo_list[0].T,
        geo_frac[0].T,
    )
    scratch = [pltpu.VMEM(operand.shape, operand.dtype) for operand in operands] + [
        pltpu.VMEM((LANES, rwidth), jnp.bfloat16),
        pltpu.VMEM((LANES, rwidth), jnp.bfloat16),
        pltpu.VMEM((LANES, rwidth), jnp.bfloat16),
        pltpu.VMEM((2 * LANES, awidth), jnp.bfloat16),
        pltpu.VMEM(((chunks + spare) * rows, 2 * LANES), jnp.bfloat16),
        pltpu.VMEM((GROUP * rows, 2 * LANES), jnp.float32),
        pltpu.VMEM(((chunks + 2) * rows, 2 * LANES), jnp.bfloat16),
        pltpu.VMEM((interp_table.shape[1], bins), jnp.float32),
        pltpu.VMEM((chunks, 2 * LANES, LANES), jnp.bfloat16),
        pltpu.VMEM((devices, rows, LANES), jnp.bfloat16),
        pltpu.VMEM((devices, rows, LANES), jnp.bfloat16),
        pltpu.VMEM((pulses, LANES), jnp.bfloat16),
        pltpu.VMEM((pulses, LANES), jnp.float32),
        pltpu.VMEM((patches, tile), jnp.float32),
        pltpu.VMEM((patches, tile), jnp.float32),
        pltpu.VMEM((patches, tile), jnp.float32),
        pltpu.VMEM((patches, tile), jnp.float32),
    ] + [pltpu.SemaphoreType.DMA((8,))] + [pltpu.SemaphoreType.DMA] * 6
    shapes = (
        jax.ShapeDtypeStruct((pulses, breadth // devices), jnp.bfloat16),
        jax.ShapeDtypeStruct((patches, tile), jnp.float32),
    )
    outside = pl.BlockSpec(memory_space=pltpu.HBM)
    return pl.pallas_call(
        functools.partial(kernel, devices, across),
        out_shape=shapes,
        in_specs=[outside] * 8,
        out_specs=(whole, whole),
        scratch_shapes=scratch,
        compiler_params=pltpu.CompilerParams(
            collective_id=0, has_side_effects=True, vmem_limit_bytes=40 * 2**20
        ),
    )(*[pltpu.with_memory_space_constraint(operand, pltpu.HBM) for operand in operands])


def solution(mesh):
    placed = (
        P(("pulse", "range"), None),
        P(),
        P(),
        P(),
        P(),
        P(),
        P(("pulse", "range"), None, None),
        P(("pulse", "range"), None, None),
    )
    return jax.shard_map(
        body,
        mesh=mesh,
        in_specs=placed,
        out_specs=(P(None, ("pulse", "range")), P(("pulse", "range"), None)),
        check_vma=False,
    )
```

```python
import functools

import jax
import jax.numpy as jnp
from jax import lax
from jax.experimental import pallas as pl
from jax.experimental.pallas import tpu as pltpu
from jax.sharding import PartitionSpec as P

LOOKS = 4
PROWS = 16
LANES = 128
GROUP = 16
BATCH = 4
MESH = pl.DeviceIdType.MESH


def iota(shape, dim):
    return lax.broadcasted_iota(jnp.int32, shape, dim)


def shifted_rows(taps, width):
    have = min(width, taps.shape[1])
    line = taps[:, :have].astype(jnp.float32)
    if have < width:
        line = jnp.concatenate([line, jnp.zeros((1, width - have), jnp.float32)], 1)
    eight = jnp.broadcast_to(line, (8, width))
    row = iota((8, width), 0)
    for bit in (1, 2, 4):
        eight = jnp.where((row & bit) != 0, pltpu.roll(eight, bit, 1), eight)
    both = jnp.concatenate([eight, pltpu.roll(eight, 8, 1)], 0).astype(jnp.bfloat16)
    tile = (16, LANES)
    for start in range(0, LANES, 16):
        moved = both if start == 0 else pltpu.roll(both, start, 1)
        keep = iota(tile, 1) >= iota(tile, 0) + start
        first = jnp.where(keep, moved[:, :LANES], jnp.zeros(tile, jnp.bfloat16))
        yield start, jnp.concatenate([first, moved[:, LANES:]], 1)


def kernel(
    devices,
    across,
    raw_in,
    rtaps_in,
    offset_in,
    band_in,
    table_in,
    ataps_in,
    list_in,
    frac_in,
    focused_ref,
    tiles_ref,
    raw_ref,
    rtaps_ref,
    offset_ref,
    band_ref,
    table_ref,
    ataps_ref,
    list_ref,
    frac_ref,
    zr_ref,
    zi_ref,
    zn_ref,
    za_ref,
    x_ref,
    sum_ref,
    f_ref,
    kernel_ref,
    b_ref,
    send_ref,
    recv_ref,
    focus_ref,
    power_ref,
    low_ref,
    high_ref,
    from_next_ref,
    from_prev_ref,
    in_sems,
    send_sem,
    recv_sem,
    low_send_sem,
    high_send_sem,
    low_recv_sem,
    high_recv_sem,
):
    pulse_at, range_at = lax.axis_index("pulse"), lax.axis_index("range")
    me = pulse_at * across + range_at
    rows, breadth = raw_ref.shape
    chunks = breadth // (2 * LANES)
    groups = chunks // GROUP
    pulses = devices * rows
    patches = list_ref.shape[1]
    rwidth = zr_ref.shape[1]
    awidth = za_ref.shape[1]

    rtaps_copy, raw_copy, offset_copy, band_copy, table_copy, ataps_copy, list_copy, frac_copy = [
        pltpu.make_async_copy(outside, inside, in_sems.at[at])
        for at, (outside, inside) in enumerate(
            (
                (rtaps_in, rtaps_ref),
                (raw_in, raw_ref),
                (offset_in, offset_ref),
                (band_in, band_ref),
                (table_in, table_ref),
                (ataps_in, ataps_ref),
                (list_in, list_ref),
                (frac_in, frac_ref),
            )
        )
    ]
    first_copies = (rtaps_copy, offset_copy, band_copy, table_copy, raw_copy)
    later_copies = (ataps_copy, list_copy, frac_copy)
    for copy in first_copies + later_copies:
        copy.start()

    def place(index):
        return (lax.div(index, across), lax.rem(index, across))

    barrier = pltpu.get_barrier_semaphore()

    def greet(distance, carry):
        other = lax.rem(me + distance, devices)
        pl.semaphore_signal(barrier, inc=1, device_id=place(other), device_id_type=MESH)
        return carry

    if groups == 1:
        for distance in range(1, devices):
            greet(distance, 0)
    else:
        lax.fori_loop(1, devices, greet, 0)

    def each_group(body):
        if groups == 1:
            body(0)
        else:
            lax.fori_loop(0, groups, lambda g, c: (body(g * GROUP), c)[1], 0)

    rtaps_copy.wait()

    for start, real_rows in shifted_rows(rtaps_ref[0:1, :], rwidth):
        zr_ref[start : start + 16, :] = real_rows
    for start, imag_rows in shifted_rows(rtaps_ref[1:2, :], rwidth):
        zi_ref[start : start + 16, :] = imag_rows
        zn_ref[start : start + 16, :] = -imag_rows

    for copy in first_copies[1:]:
        copy.wait()

    side = (2 * LANES, 2 * LANES)
    column = iota(side, 1)
    source = 2 * (LANES - 1 - (column % LANES)) + column // LANES
    parts_apart = (iota(side, 0) == source).astype(jnp.float32).astype(jnp.bfloat16)
    lines = jnp.concatenate(
        [raw_ref[:, 2 * LANES * j : 2 * LANES * (j + 1)] for j in range(chunks)], 0
    )
    x_ref[0 : chunks * rows, :] = jnp.dot(
        lines, parts_apart, preferred_element_type=jnp.float32
    ).astype(jnp.bfloat16)
    spare = x_ref.shape[0] - chunks * rows
    if spare:
        x_ref[chunks * rows :, :] = jnp.zeros((spare, 2 * LANES), jnp.bfloat16)

    bands, bins = table_ref.shape[1], chunks * LANES
    onehot = (iota((bands, bins), 0) == band_ref[...]).astype(jnp.float32).astype(jnp.bfloat16)
    kernel_ref[...] = jnp.dot(table_ref[...], onehot, preferred_element_type=jnp.float32)
    window = (2 * LANES, LANES)
    lane = iota(window, 0) % LANES
    shift = jnp.where(lane < LANES // 2, -LANES, LANES)
    bin_of = LANES - 1 - lane + jnp.where(iota(window, 0) < LANES, 0, shift)
    delta = (bin_of - iota(window, 1) + 3).astype(jnp.int16)

    def band_matrix(chunk):
        at = pl.ds(pl.multiple_of(chunk * LANES, LANES), LANES)
        offsets = jnp.broadcast_to(offset_ref[:, at], (16, LANES)).astype(jnp.int16)
        distance = delta - jnp.broadcast_to(offsets[0:1], window)
        weights = kernel_ref[:, at]
        banded = jnp.zeros(window, jnp.bfloat16)
        for tap in range(weights.shape[0]):
            weight = jnp.broadcast_to(weights[tap : tap + 1], (16, LANES)).astype(jnp.bfloat16)
            weight = jnp.broadcast_to(weight[0:1], window)
            banded = jnp.where(distance == jnp.int16(tap), weight, banded)
        b_ref[chunk] = banded

    def range_group(first):
        for apart in range(rwidth // LANES):
            count = GROUP - apart if groups == 1 else GROUP
            if apart < GROUP:
                band_matrix(first + apart)
            if count <= 0:
                continue
            at = slice(LANES * apart, LANES * (apart + 1))
            zr, zi, zn = zr_ref[:, at], zi_ref[:, at], zn_ref[:, at]
            weights = jnp.concatenate(
                [jnp.concatenate([zr, zi], 1), jnp.concatenate([zn, zr], 1)], 0
            )
            start = pl.multiple_of((first + apart) * rows, 16)
            product = jnp.dot(
                x_ref[pl.ds(start, count * rows), :],
                weights,
                preferred_element_type=jnp.float32,
            )
            if apart == 0:
                sum_ref[...] = product
            else:
                sum_ref[0 : count * rows, :] += product
        start = pl.multiple_of((first + 1) * rows, 16)
        f_ref[pl.ds(start, GROUP * rows), :] = sum_ref[...].astype(jnp.bfloat16)

    f_ref[0:rows, :] = jnp.zeros((rows, 2 * LANES), jnp.bfloat16)
    f_ref[(chunks + 1) * rows :, :] = jnp.zeros((rows, 2 * LANES), jnp.bfloat16)
    each_group(range_group)

    left = iota((rows, LANES), 1) < LANES // 2

    def migrate_group(first):
        ahead = list(range(1, GROUP, 2)) + list(range(2, GROUP + 1, 2))
        chunk_at = [lax.rem(lax.div(me, 2) + first + step, chunks) for step in ahead]

        def migrated(chunk):
            start = pl.multiple_of(chunk * rows, 16)
            before = f_ref[pl.ds(start, rows), :]
            here = f_ref[pl.ds(pl.multiple_of(start + rows, 16), rows), :]
            after = f_ref[pl.ds(pl.multiple_of(start + 2 * rows, 16), rows), :]
            both = []
            for part in (slice(0, LANES), slice(LANES, 2 * LANES)):
                around = jnp.where(left, before[:, part], after[:, part])
                both.append(jnp.concatenate([here[:, part], around], 1))
            moved = jnp.dot(
                jnp.concatenate(both, 0), b_ref[chunk], preferred_element_type=jnp.float32
            )
            real_part, imag_part = moved[:rows], moved[rows:]
            even = jnp.where(left, real_part, pltpu.roll(imag_part, LANES // 2, 1))
            odd = jnp.where(left, pltpu.roll(real_part, LANES // 2, 1), imag_part)
            return even.astype(jnp.bfloat16), odd.astype(jnp.bfloat16)

        later = [migrated(chunk) for chunk in chunk_at[:BATCH]]
        for at in range(0, GROUP, BATCH):
            now = later
            later = [migrated(chunk) for chunk in chunk_at[at + BATCH : at + 2 * BATCH]]
            batch = list(enumerate(chunk_at))[at : at + BATCH]
            for (j, chunk), pair in zip(batch, now):
                for half in range(2):
                    send_ref[2 * chunk + half] = pair[half]
            if groups == 1 and at == 0:
                pl.semaphore_wait(barrier, devices - 1)
            for j, chunk in batch:
                for half in range(2):
                    send(2 * chunk + half, groups > 1 or j == GROUP - 1)

    def send(other, own_possible):
        def go():
            pltpu.make_async_remote_copy(
                src_ref=send_ref.at[other],
                dst_ref=recv_ref.at[me],
                send_sem=send_sem,
                recv_sem=recv_sem,
                device_id=place(other),
                device_id_type=MESH,
            ).start()

        if own_possible:
            pl.when(other != me)(go)
        else:
            go()

    if groups > 1:
        pl.semaphore_wait(barrier, devices - 1)
    each_group(migrate_group)
    recv_ref[me] = send_ref[me]

    for copy in later_copies:
        copy.wait()
    for part in range(2):
        for start, moved_rows in shifted_rows(ataps_ref[part : part + 1, :], awidth):
            at = LANES * part + start
            za_ref[at : at + 16, :] = moved_rows

    base = (me - 1) * patches
    slot = iota((3 * patches, patches), 0) + base
    spread = jnp.zeros((3 * patches, patches), jnp.float32)
    for over in range(list_ref.shape[0]):
        spread += jnp.where(
            list_ref[over : over + 1, :] == slot, frac_ref[over : over + 1, :], 0.0
        )

    square = (LANES, LANES)
    column = iota(square, 1)
    parts_beside = (iota(square, 0) == LANES // 2 * (column % 2) + column // 2)
    parts_beside = parts_beside.astype(jnp.float32).astype(jnp.bfloat16)
    sign = jnp.where(iota(square, 1) < LANES // 2, -1.0, 1.0)

    others = pl.ds(0, devices - 1)
    pltpu.make_async_copy(recv_ref.at[others], recv_ref.at[others], recv_sem).wait()

    for block in range(pulses // LANES):
        depth = min(awidth, pulses - LANES * block)
        first = LANES * block // rows
        columns = recv_ref[first : first + depth // rows].reshape(depth, LANES)
        product = jnp.dot(za_ref[:, :depth], columns, preferred_element_type=jnp.float32)
        focus = product[:LANES] + sign * pltpu.roll(product[LANES:], LANES // 2, 1)
        at = slice(LANES * block, LANES * (block + 1))
        focus_ref[at, :] = focus.astype(jnp.bfloat16)
        power_ref[at, :] = focus * focus

    stride = LOOKS * PROWS
    left_half = iota((patches, LANES), 1) < LANES // 2
    pieces = []
    for piece in range(stride // (2 * LOOKS)):
        summed = []
        for half in range(2):
            start = 2 * LOOKS * piece + LOOKS * half
            total = power_ref[pl.ds(start, patches, stride=stride), :]
            for look in range(1, LOOKS):
                total += power_ref[pl.ds(start + look, patches, stride=stride), :]
            summed.append(total + pltpu.roll(total, LANES // 2, 1))
        pieces.append(jnp.where(left_half, summed[0], summed[1]) * (1.0 / LOOKS))
    looked = jnp.concatenate(pieces, 1)

    def tile_sums(first):
        weights = spread[first : first + patches]
        total = weights[:, 0:1] * looked[0:1, :]
        for patch in range(1, patches):
            total += weights[:, patch : patch + 1] * looked[patch : patch + 1, :]
        return total

    low_ref[...] = tile_sums(0)
    high_ref[...] = tile_sums(2 * patches)

    def low_copy():
        return pltpu.make_async_remote_copy(
            src_ref=low_ref,
            dst_ref=from_next_ref,
            send_sem=low_send_sem,
            recv_sem=low_recv_sem,
            device_id=place(jnp.maximum(me - 1, 0)),
            device_id_type=MESH,
        )

    def high_copy():
        return pltpu.make_async_remote_copy(
            src_ref=high_ref,
            dst_ref=from_prev_ref,
            send_sem=high_send_sem,
            recv_sem=high_recv_sem,
            device_id=place(jnp.minimum(me + 1, devices - 1)),
            device_id_type=MESH,
        )

    @pl.when(me > 0)
    def _():
        low_copy().start()

    @pl.when(me < devices - 1)
    def _():
        high_copy().start()

    tiles_ref[...] = tile_sums(patches)
    focused_ref[...] = jnp.dot(
        focus_ref[...], parts_beside, preferred_element_type=jnp.float32
    ).astype(jnp.bfloat16)
    pltpu.make_async_copy(send_ref.at[others], send_ref.at[others], send_sem).wait()

    @pl.when(me < devices - 1)
    def _():
        low_copy().wait_recv()
        tiles_ref[...] += from_next_ref[...]

    @pl.when(me > 0)
    def _():
        high_copy().wait_recv()
        tiles_ref[...] += from_prev_ref[...]

    @pl.when(me > 0)
    def _():
        low_copy().wait_send()

    @pl.when(me < devices - 1)
    def _():
        high_copy().wait_send()


def body(
    raw_echoes, range_taps, mig_offset, interp_band, interp_table, azimuth_taps, geo_list, geo_frac
):
    across = lax.axis_size("range")
    devices = lax.axis_size("pulse") * across
    rows, breadth = raw_echoes.shape
    pulses = rows * devices
    bins = breadth // 2
    chunks = bins // LANES
    patches = geo_list.shape[1]
    tile = PROWS * (bins // devices)
    rwidth = min(bins, range_taps.shape[0] + LANES)
    awidth = min(pulses, azimuth_taps.shape[0] + LANES)
    spare = 0 if chunks == GROUP else rwidth // LANES
    whole = pl.BlockSpec(memory_space=pltpu.VMEM)
    operands = (
        raw_echoes,
        range_taps.T,
        mig_offset.reshape(1, bins),
        interp_band.reshape(1, bins),
        interp_table.T,
        azimuth_taps.T,
        geo_list[0].T,
        geo_frac[0].T,
    )
    scratch = [pltpu.VMEM(operand.shape, operand.dtype) for operand in operands] + [
        pltpu.VMEM((LANES, rwidth), jnp.bfloat16),
        pltpu.VMEM((LANES, rwidth), jnp.bfloat16),
        pltpu.VMEM((LANES, rwidth), jnp.bfloat16),
        pltpu.VMEM((2 * LANES, awidth), jnp.bfloat16),
        pltpu.VMEM(((chunks + spare) * rows, 2 * LANES), jnp.bfloat16),
        pltpu.VMEM((GROUP * rows, 2 * LANES), jnp.float32),
        pltpu.VMEM(((chunks + 2) * rows, 2 * LANES), jnp.bfloat16),
        pltpu.VMEM((interp_table.shape[1], bins), jnp.float32),
        pltpu.VMEM((chunks, 2 * LANES, LANES), jnp.bfloat16),
        pltpu.VMEM((devices, rows, LANES), jnp.bfloat16),
        pltpu.VMEM((devices, rows, LANES), jnp.bfloat16),
        pltpu.VMEM((pulses, LANES), jnp.bfloat16),
        pltpu.VMEM((pulses, LANES), jnp.float32),
        pltpu.VMEM((patches, tile), jnp.float32),
        pltpu.VMEM((patches, tile), jnp.float32),
        pltpu.VMEM((patches, tile), jnp.float32),
        pltpu.VMEM((patches, tile), jnp.float32),
    ] + [pltpu.SemaphoreType.DMA((8,))] + [pltpu.SemaphoreType.DMA] * 6
    shapes = (
        jax.ShapeDtypeStruct((pulses, breadth // devices), jnp.bfloat16),
        jax.ShapeDtypeStruct((patches, tile), jnp.float32),
    )
    outside = pl.BlockSpec(memory_space=pltpu.HBM)
    return pl.pallas_call(
        functools.partial(kernel, devices, across),
        out_shape=shapes,
        in_specs=[outside] * 8,
        out_specs=(whole, whole),
        scratch_shapes=scratch,
        compiler_params=pltpu.CompilerParams(
            collective_id=0, has_side_effects=True, vmem_limit_bytes=40 * 2**20
        ),
    )(*[pltpu.with_memory_space_constraint(operand, pltpu.HBM) for operand in operands])


def solution(mesh):
    placed = (
        P(("pulse", "range"), None),
        P(),
        P(),
        P(),
        P(),
        P(),
        P(("pulse", "range"), None, None),
        P(("pulse", "range"), None, None),
    )
    return jax.shard_map(
        body,
        mesh=mesh,
        in_specs=placed,
        out_specs=(P(None, ("pulse", "range")), P(("pulse", "range"), None)),
        check_vma=False,
    )
```

```python
import functools

import jax
import jax.numpy as jnp
from jax import lax
from jax.experimental import pallas as pl
from jax.experimental.pallas import tpu as pltpu
from jax.sharding import PartitionSpec as P

LOOKS = 4
PROWS = 16
LANES = 128
GROUP = 16
BATCH = 4
MESH = pl.DeviceIdType.MESH


def iota(shape, dim):
    return lax.broadcasted_iota(jnp.int32, shape, dim)


def shifted_rows(taps, width, stride, step):
    have = min(width, taps.shape[1])
    line = taps[:, :have].astype(jnp.float32)
    if have < width:
        line = jnp.concatenate([line, jnp.zeros((1, width - have), jnp.float32)], 1)
    eight = jnp.broadcast_to(line, (8, width))
    row = iota((8, width), 0)
    for bit in (1, 2, 4):
        eight = jnp.where((row & bit) != 0, pltpu.roll(eight, bit * stride, 1), eight)
    both = jnp.concatenate([eight, pltpu.roll(eight, 8 * stride, 1)], 0).astype(jnp.bfloat16)
    tile = (16, LANES)
    for part in range(LANES // 16):
        moved = both if part == 0 else pltpu.roll(both, step * part, 1)
        keep = iota(tile, 1) >= iota(tile, 0) * stride + step * part
        first = jnp.where(keep, moved[:, :LANES], jnp.zeros(tile, jnp.bfloat16))
        yield 16 * part, jnp.concatenate([first, moved[:, LANES:]], 1)


def kernel(
    devices,
    across,
    raw_in,
    rtaps_in,
    offset_in,
    band_in,
    table_in,
    ataps_in,
    list_in,
    frac_in,
    focused_ref,
    tiles_ref,
    raw_ref,
    rtaps_ref,
    offset_ref,
    band_ref,
    table_ref,
    ataps_ref,
    list_ref,
    frac_ref,
    zr_ref,
    zi_ref,
    zn_ref,
    za_ref,
    x_ref,
    sum_ref,
    f_ref,
    kernel_ref,
    b_ref,
    send_ref,
    recv_ref,
    focus_ref,
    focus_sum_ref,
    looked_ref,
    low_ref,
    high_ref,
    from_next_ref,
    from_prev_ref,
    in_sems,
    send_sem,
    recv_sems,
    low_send_sem,
    high_send_sem,
    low_recv_sem,
    high_recv_sem,
):
    pulse_at, range_at = lax.axis_index("pulse"), lax.axis_index("range")
    me = pulse_at * across + range_at
    rows, breadth = raw_ref.shape
    chunks = breadth // (2 * LANES)
    groups = chunks // GROUP
    pulses = devices * rows
    patches = list_ref.shape[1]
    sources = LANES // rows
    blocks = pulses // LANES
    rwidth = zr_ref.shape[1]
    awidth = za_ref.shape[1]

    rtaps_copy, raw_copy, offset_copy, band_copy, table_copy, ataps_copy, list_copy, frac_copy = [
        pltpu.make_async_copy(outside, inside, in_sems.at[at])
        for at, (outside, inside) in enumerate(
            (
                (rtaps_in, rtaps_ref),
                (raw_in, raw_ref),
                (offset_in, offset_ref),
                (band_in, band_ref),
                (table_in, table_ref),
                (ataps_in, ataps_ref),
                (list_in, list_ref),
                (frac_in, frac_ref),
            )
        )
    ]
    first_copies = (rtaps_copy, offset_copy, band_copy, table_copy, raw_copy)
    later_copies = (ataps_copy, list_copy, frac_copy)
    rtaps_copy.start()
    raw_copy.start()

    def place(index):
        return (lax.div(index, across), lax.rem(index, across))

    barrier = pltpu.get_barrier_semaphore()

    def greet(distance, carry):
        other = lax.rem(me + distance, devices)
        pl.semaphore_signal(barrier, inc=1, device_id=place(other), device_id_type=MESH)
        return carry

    if groups == 1:
        for distance in range(1, devices):
            greet(distance, 0)
    else:
        lax.fori_loop(1, devices, greet, 0)
    for copy in (offset_copy, band_copy, table_copy) + later_copies:
        copy.start()

    def each_group(body):
        if groups == 1:
            body(0)
        else:
            lax.fori_loop(0, groups, lambda g, c: (body(g * GROUP), c)[1], 0)

    rtaps_copy.wait()

    for start, real_rows in shifted_rows(rtaps_ref[0:1, :], rwidth, 1, 16):
        zr_ref[start : start + 16, :] = real_rows
    for start, imag_rows in shifted_rows(rtaps_ref[1:2, :], rwidth, 1, 16):
        zi_ref[start : start + 16, :] = imag_rows
        zn_ref[start : start + 16, :] = -imag_rows

    for copy in first_copies[1:]:
        copy.wait()

    side = (2 * LANES, 2 * LANES)
    column = iota(side, 1)
    source = 2 * (LANES - 1 - (column % LANES)) + column // LANES
    parts_apart = (iota(side, 0) == source).astype(jnp.float32).astype(jnp.bfloat16)
    lines = jnp.concatenate(
        [raw_ref[:, 2 * LANES * j : 2 * LANES * (j + 1)] for j in range(chunks)], 0
    )
    x_ref[0 : chunks * rows, :] = jnp.dot(
        lines, parts_apart, preferred_element_type=jnp.float32
    ).astype(jnp.bfloat16)
    spare = x_ref.shape[0] - chunks * rows
    if spare:
        x_ref[chunks * rows :, :] = jnp.zeros((spare, 2 * LANES), jnp.bfloat16)

    bands, bins = table_ref.shape[1], chunks * LANES
    onehot = (iota((bands, bins), 0) == band_ref[...]).astype(jnp.float32).astype(jnp.bfloat16)
    kernel_ref[...] = jnp.dot(table_ref[...], onehot, preferred_element_type=jnp.float32)
    window = (2 * LANES, LANES)
    lane = iota(window, 0) % LANES
    shift = jnp.where(lane < LANES // 2, -LANES, LANES)
    bin_of = LANES - 1 - lane + jnp.where(iota(window, 0) < LANES, 0, shift)
    delta = (bin_of - iota(window, 1) + 3).astype(jnp.int16)

    def band_matrix(chunk):
        at = pl.ds(pl.multiple_of(chunk * LANES, LANES), LANES)
        offsets = jnp.broadcast_to(offset_ref[:, at], (16, LANES)).astype(jnp.int16)
        distance = delta - jnp.concatenate([offsets] * (2 * LANES // 16), 0)
        weights = kernel_ref[:, at]
        banded = jnp.zeros(window, jnp.bfloat16)
        for tap in range(weights.shape[0]):
            weight = jnp.broadcast_to(weights[tap : tap + 1], (16, LANES)).astype(jnp.bfloat16)
            weight = jnp.concatenate([weight] * (2 * LANES // 16), 0)
            banded = jnp.where(distance == jnp.int16(tap), weight, banded)
        b_ref[chunk] = banded

    def range_group(first):
        for apart in range(rwidth // LANES):
            count = GROUP - apart if groups == 1 else GROUP
            if apart < GROUP:
                band_matrix(first + apart)
            if count <= 0:
                continue
            at = slice(LANES * apart, LANES * (apart + 1))
            zr, zi, zn = zr_ref[:, at], zi_ref[:, at], zn_ref[:, at]
            weights = jnp.concatenate(
                [jnp.concatenate([zr, zi], 1), jnp.concatenate([zn, zr], 1)], 0
            )
            start = pl.multiple_of((first + apart) * rows, 16)
            product = jnp.dot(
                x_ref[pl.ds(start, count * rows), :],
                weights,
                preferred_element_type=jnp.float32,
            )
            if apart == 0:
                sum_ref[...] = product
            else:
                sum_ref[0 : count * rows, :] += product
        start = pl.multiple_of((first + 1) * rows, 16)
        f_ref[pl.ds(start, GROUP * rows), :] = sum_ref[...].astype(jnp.bfloat16)

    f_ref[0:rows, :] = jnp.zeros((rows, 2 * LANES), jnp.bfloat16)
    f_ref[(chunks + 1) * rows :, :] = jnp.zeros((rows, 2 * LANES), jnp.bfloat16)
    each_group(range_group)

    left = iota((rows, LANES), 1) < LANES // 2

    def migrate_group(first):
        ahead = list(range(1, GROUP, 2)) + list(range(2, GROUP + 1, 2))
        chunk_at = [lax.rem(lax.div(me, 2) + first + step, chunks) for step in ahead]

        def migrated(chunk):
            start = pl.multiple_of(chunk * rows, 16)
            before = f_ref[pl.ds(start, rows), :]
            here = f_ref[pl.ds(pl.multiple_of(start + rows, 16), rows), :]
            after = f_ref[pl.ds(pl.multiple_of(start + 2 * rows, 16), rows), :]
            both = []
            for part in (slice(0, LANES), slice(LANES, 2 * LANES)):
                around = jnp.where(left, before[:, part], after[:, part])
                both.append(jnp.concatenate([here[:, part], around], 1))
            moved = jnp.dot(
                jnp.concatenate(both, 0), b_ref[chunk], preferred_element_type=jnp.float32
            )
            real_part, imag_part = moved[:rows], moved[rows:]
            even = jnp.where(left, real_part, pltpu.roll(imag_part, LANES // 2, 1))
            odd = jnp.where(left, pltpu.roll(real_part, LANES // 2, 1), imag_part)
            return even.astype(jnp.bfloat16), odd.astype(jnp.bfloat16)

        later = [migrated(chunk) for chunk in chunk_at[:BATCH]]
        for at in range(0, GROUP, BATCH):
            now = later
            later = [migrated(chunk) for chunk in chunk_at[at + BATCH : at + 2 * BATCH]]
            batch = list(enumerate(chunk_at))[at : at + BATCH]
            for (j, chunk), pair in zip(batch, now):
                for half in range(2):
                    send_ref[2 * chunk + half] = pair[half]
            if groups == 1 and at == 0:
                pl.semaphore_wait(barrier, devices - 1)
            for j, chunk in batch:
                for half in range(2):
                    send(2 * chunk + half, groups > 1 or j == GROUP - 1)

    def send(other, own_possible):
        def go():
            pltpu.make_async_remote_copy(
                src_ref=send_ref.at[other],
                dst_ref=recv_ref.at[me],
                send_sem=send_sem,
                recv_sem=recv_sems.at[lax.div(me, sources)],
                device_id=place(other),
                device_id_type=MESH,
            ).start()

        if own_possible:
            pl.when(other != me)(go)
        else:
            go()

    if groups > 1:
        pl.semaphore_wait(barrier, devices - 1)
    each_group(migrate_group)
    own_copy = pltpu.make_async_copy(
        send_ref.at[me], recv_ref.at[me], recv_sems.at[lax.div(me, sources)]
    )
    own_copy.start()

    for copy in later_copies:
        copy.wait()
    for part in range(2):
        for start, moved_rows in shifted_rows(ataps_ref[part : part + 1, :], awidth, 8, 1):
            at = LANES * part + start
            za_ref[at : at + 16, :] = moved_rows

    base = (me - 1) * patches
    slot = iota((3 * patches, patches), 0) + base
    spread = jnp.zeros((3 * patches, patches), jnp.float32)
    for over in range(list_ref.shape[0]):
        spread += jnp.where(
            list_ref[over : over + 1, :] == slot, frac_ref[over : over + 1, :], 0.0
        )

    square = (LANES, LANES)
    column = iota(square, 1)
    parts_beside = (iota(square, 0) == LANES // 2 * (column % 2) + column // 2)
    parts_beside = parts_beside.astype(jnp.float32).astype(jnp.bfloat16)
    sign = jnp.where(iota(square, 1) < LANES // 2, -1.0, 1.0)

    for block in range(blocks):
        at = pl.ds(sources * block, sources)
        pltpu.make_async_copy(recv_ref.at[at], recv_ref.at[at], recv_sems.at[block]).wait()
        columns = recv_ref[sources * block : sources * (block + 1)].reshape(LANES, LANES)
        for apart in range(min(block + 1, awidth // LANES)):
            product = jnp.dot(
                za_ref[:, LANES * apart : LANES * (apart + 1)],
                columns,
                preferred_element_type=jnp.float32,
            )
            if apart == 0:
                focus_sum_ref[block] = product
            else:
                focus_sum_ref[block - apart] += product

    left_half = iota((LANES // 8, LANES), 1) < LANES // 2
    for block in range(blocks):
        product = focus_sum_ref[block]
        focus = product[:LANES] + sign * pltpu.roll(product[LANES:], LANES // 2, 1)
        focus_ref[LANES * block : LANES * (block + 1), :] = focus.astype(jnp.bfloat16)
        power = (focus * focus).reshape(2, LOOKS, LANES // 8, LANES)
        summed = []
        for half in range(2):
            total = power[half, 0]
            for look in range(1, LOOKS):
                total += power[half, look]
            summed.append(total + pltpu.roll(total, LANES // 2, 1))
        looked_ref[LANES // 8 * block : LANES // 8 * (block + 1), :] = jnp.where(
            left_half, summed[0], summed[1]
        ) * (1.0 / LOOKS)
    stride = LOOKS * PROWS // 8
    pieces = [looked_ref[pl.ds(piece, patches, stride=stride), :] for piece in range(stride)]
    looked = jnp.concatenate(pieces, 1)

    def tile_sums(first):
        weights = spread[first : first + patches]
        total = weights[:, 0:1] * looked[0:1, :]
        for patch in range(1, patches):
            total += weights[:, patch : patch + 1] * looked[patch : patch + 1, :]
        return total

    low_ref[...] = tile_sums(0)
    high_ref[...] = tile_sums(2 * patches)

    def low_copy():
        return pltpu.make_async_remote_copy(
            src_ref=low_ref,
            dst_ref=from_next_ref,
            send_sem=low_send_sem,
            recv_sem=low_recv_sem,
            device_id=place(jnp.maximum(me - 1, 0)),
            device_id_type=MESH,
        )

    def high_copy():
        return pltpu.make_async_remote_copy(
            src_ref=high_ref,
            dst_ref=from_prev_ref,
            send_sem=high_send_sem,
            recv_sem=high_recv_sem,
            device_id=place(jnp.minimum(me + 1, devices - 1)),
            device_id_type=MESH,
        )

    @pl.when(me > 0)
    def _():
        low_copy().start()

    @pl.when(me < devices - 1)
    def _():
        high_copy().start()

    tiles_ref[...] = tile_sums(patches)
    row = iota(square, 0)
    in_order = (column == row % 8 * (LANES // 8) + row // 8).astype(jnp.float32)
    in_order = in_order.astype(jnp.bfloat16)
    for block in range(blocks):
        at = slice(LANES * block, LANES * (block + 1))
        ordered = jnp.dot(in_order, focus_ref[at, :], preferred_element_type=jnp.float32)
        focused_ref[at, :] = jnp.dot(
            ordered.astype(jnp.bfloat16), parts_beside, preferred_element_type=jnp.float32
        ).astype(jnp.bfloat16)
    others = pl.ds(0, devices - 1)
    pltpu.make_async_copy(send_ref.at[others], send_ref.at[others], send_sem).wait()

    @pl.when(me < devices - 1)
    def _():
        low_copy().wait_recv()
        tiles_ref[...] += from_next_ref[...]

    @pl.when(me > 0)
    def _():
        high_copy().wait_recv()
        tiles_ref[...] += from_prev_ref[...]

    @pl.when(me > 0)
    def _():
        low_copy().wait_send()

    @pl.when(me < devices - 1)
    def _():
        high_copy().wait_send()


def body(
    raw_echoes, range_taps, mig_offset, interp_band, interp_table, azimuth_taps, geo_list, geo_frac
):
    across = lax.axis_size("range")
    devices = lax.axis_size("pulse") * across
    rows, breadth = raw_echoes.shape
    pulses = rows * devices
    bins = breadth // 2
    chunks = bins // LANES
    patches = geo_list.shape[1]
    tile = PROWS * (bins // devices)
    rwidth = min(bins, range_taps.shape[0] + LANES)
    awidth = min(pulses, azimuth_taps.shape[0] + LANES)
    spare = 0 if chunks == GROUP else rwidth // LANES
    whole = pl.BlockSpec(memory_space=pltpu.VMEM)
    operands = (
        raw_echoes,
        range_taps.T,
        mig_offset.reshape(1, bins),
        interp_band.reshape(1, bins),
        interp_table.T,
        azimuth_taps.T,
        geo_list[0].T,
        geo_frac[0].T,
    )
    scratch = [pltpu.VMEM(operand.shape, operand.dtype) for operand in operands] + [
        pltpu.VMEM((LANES, rwidth), jnp.bfloat16),
        pltpu.VMEM((LANES, rwidth), jnp.bfloat16),
        pltpu.VMEM((LANES, rwidth), jnp.bfloat16),
        pltpu.VMEM((2 * LANES, awidth), jnp.bfloat16),
        pltpu.VMEM(((chunks + spare) * rows, 2 * LANES), jnp.bfloat16),
        pltpu.VMEM((GROUP * rows, 2 * LANES), jnp.float32),
        pltpu.VMEM(((chunks + 2) * rows, 2 * LANES), jnp.bfloat16),
        pltpu.VMEM((interp_table.shape[1], bins), jnp.float32),
        pltpu.VMEM((chunks, 2 * LANES, LANES), jnp.bfloat16),
        pltpu.VMEM((devices, rows, LANES), jnp.bfloat16),
        pltpu.VMEM((devices, rows, LANES), jnp.bfloat16),
        pltpu.VMEM((pulses, LANES), jnp.bfloat16),
        pltpu.VMEM((pulses // LANES, 2 * LANES, LANES), jnp.float32),
        pltpu.VMEM((pulses // 8, LANES), jnp.float32),
        pltpu.VMEM((patches, tile), jnp.float32),
        pltpu.VMEM((patches, tile), jnp.float32),
        pltpu.VMEM((patches, tile), jnp.float32),
        pltpu.VMEM((patches, tile), jnp.float32),
    ] + [
        pltpu.SemaphoreType.DMA((8,)),
        pltpu.SemaphoreType.DMA,
        pltpu.SemaphoreType.DMA((pulses // LANES,)),
    ] + [pltpu.SemaphoreType.DMA] * 4
    shapes = (
        jax.ShapeDtypeStruct((pulses, breadth // devices), jnp.bfloat16),
        jax.ShapeDtypeStruct((patches, tile), jnp.float32),
    )
    outside = pl.BlockSpec(memory_space=pltpu.HBM)
    return pl.pallas_call(
        functools.partial(kernel, devices, across),
        out_shape=shapes,
        in_specs=[outside] * 8,
        out_specs=(whole, whole),
        scratch_shapes=scratch,
        compiler_params=pltpu.CompilerParams(
            collective_id=0, has_side_effects=True, vmem_limit_bytes=40 * 2**20
        ),
    )(*[pltpu.with_memory_space_constraint(operand, pltpu.HBM) for operand in operands])


def solution(mesh):
    placed = (
        P(("pulse", "range"), None),
        P(),
        P(),
        P(),
        P(),
        P(),
        P(("pulse", "range"), None, None),
        P(("pulse", "range"), None, None),
    )
    return jax.shard_map(
        body,
        mesh=mesh,
        in_specs=placed,
        out_specs=(P(None, ("pulse", "range")), P(("pulse", "range"), None)),
        check_vma=False,
    )
```

```python
import functools

import jax
import jax.numpy as jnp
from jax import lax
from jax.experimental import pallas as pl
from jax.experimental.pallas import tpu as pltpu
from jax.sharding import PartitionSpec as P

LOOKS = 4
PROWS = 16
LANES = 128
GROUP = 16
BATCH = 16
MESH = pl.DeviceIdType.MESH


def iota(shape, dim):
    return lax.broadcasted_iota(jnp.int32, shape, dim)


def shifted_rows(taps, width, stride, step):
    have = min(width, taps.shape[1])
    line = taps[:, :have].astype(jnp.float32)
    if have < width:
        line = jnp.concatenate([line, jnp.zeros((1, width - have), jnp.float32)], 1)
    eight = jnp.broadcast_to(line, (8, width))
    row = iota((8, width), 0)
    for bit in (1, 2, 4):
        eight = jnp.where((row & bit) != 0, pltpu.roll(eight, bit * stride, 1), eight)
    both = jnp.concatenate([eight, pltpu.roll(eight, 8 * stride, 1)], 0).astype(jnp.bfloat16)
    tile = (16, LANES)
    for part in range(LANES // 16):
        moved = both if part == 0 else pltpu.roll(both, step * part, 1)
        keep = iota(tile, 1) >= iota(tile, 0) * stride + step * part
        first = jnp.where(keep, moved[:, :LANES], jnp.zeros(tile, jnp.bfloat16))
        yield 16 * part, jnp.concatenate([first, moved[:, LANES:]], 1)


def kernel(
    devices,
    across,
    raw_in,
    rtaps_in,
    offset_in,
    band_in,
    table_in,
    ataps_in,
    list_in,
    frac_in,
    focused_ref,
    tiles_ref,
    raw_ref,
    rtaps_ref,
    offset_ref,
    band_ref,
    table_ref,
    ataps_ref,
    list_ref,
    frac_ref,
    zr_ref,
    zi_ref,
    zn_ref,
    za_ref,
    x_ref,
    sum_ref,
    f_ref,
    kernel_ref,
    b_ref,
    send_ref,
    recv_ref,
    focus_ref,
    focus_sum_ref,
    looked_ref,
    low_ref,
    high_ref,
    from_next_ref,
    from_prev_ref,
    in_sems,
    send_sem,
    recv_sems,
    low_send_sem,
    high_send_sem,
    low_recv_sem,
    high_recv_sem,
):
    pulse_at, range_at = lax.axis_index("pulse"), lax.axis_index("range")
    me = pulse_at * across + range_at
    rows, breadth = raw_ref.shape
    chunks = breadth // (2 * LANES)
    groups = chunks // GROUP
    pulses = devices * rows
    patches = list_ref.shape[1]
    sources = LANES // rows
    blocks = pulses // LANES
    rwidth = zr_ref.shape[1]
    awidth = za_ref.shape[1]

    rtaps_copy, raw_copy, offset_copy, band_copy, table_copy, ataps_copy, list_copy, frac_copy = [
        pltpu.make_async_copy(outside, inside, in_sems.at[at])
        for at, (outside, inside) in enumerate(
            (
                (rtaps_in, rtaps_ref),
                (raw_in, raw_ref),
                (offset_in, offset_ref),
                (band_in, band_ref),
                (table_in, table_ref),
                (ataps_in, ataps_ref),
                (list_in, list_ref),
                (frac_in, frac_ref),
            )
        )
    ]
    first_copies = (rtaps_copy, offset_copy, band_copy, table_copy, raw_copy)
    later_copies = (ataps_copy, list_copy, frac_copy)
    rtaps_copy.start()
    raw_copy.start()

    def place(index):
        return (lax.div(index, across), lax.rem(index, across))

    barrier = pltpu.get_barrier_semaphore()

    def greet(distance, carry):
        other = lax.rem(me + distance, devices)
        pl.semaphore_signal(barrier, inc=1, device_id=place(other), device_id_type=MESH)
        return carry

    if groups == 1:
        for distance in range(1, devices):
            greet(distance, 0)
    else:
        lax.fori_loop(1, devices, greet, 0)
    for copy in (offset_copy, band_copy, table_copy) + later_copies:
        copy.start()

    def each_group(body):
        if groups == 1:
            body(0)
        else:
            lax.fori_loop(0, groups, lambda g, c: (body(g * GROUP), c)[1], 0)

    rtaps_copy.wait()

    for start, real_rows in shifted_rows(rtaps_ref[0:1, :], rwidth, 1, 16):
        zr_ref[start : start + 16, :] = real_rows
    for start, imag_rows in shifted_rows(rtaps_ref[1:2, :], rwidth, 1, 16):
        zi_ref[start : start + 16, :] = imag_rows
        zn_ref[start : start + 16, :] = -imag_rows

    for copy in first_copies[1:]:
        copy.wait()

    side = (2 * LANES, 2 * LANES)
    column = iota(side, 1)
    source = 2 * (LANES - 1 - (column % LANES)) + column // LANES
    parts_apart = (iota(side, 0) == source).astype(jnp.float32).astype(jnp.bfloat16)
    lines = jnp.concatenate(
        [raw_ref[:, 2 * LANES * j : 2 * LANES * (j + 1)] for j in range(chunks)], 0
    )
    x_ref[0 : chunks * rows, :] = jnp.dot(
        lines, parts_apart, preferred_element_type=jnp.float32
    ).astype(jnp.bfloat16)
    spare = x_ref.shape[0] - chunks * rows
    if spare:
        x_ref[chunks * rows :, :] = jnp.zeros((spare, 2 * LANES), jnp.bfloat16)

    bands, bins = table_ref.shape[1], chunks * LANES
    onehot = (iota((bands, bins), 0) == band_ref[...]).astype(jnp.float32).astype(jnp.bfloat16)
    kernel_ref[...] = jnp.dot(table_ref[...], onehot, preferred_element_type=jnp.float32)
    window = (2 * LANES, LANES)
    lane = iota(window, 0) % LANES
    shift = jnp.where(lane < LANES // 2, -LANES, LANES)
    bin_of = LANES - 1 - lane + jnp.where(iota(window, 0) < LANES, 0, shift)
    delta = (bin_of - iota(window, 1) + 3).astype(jnp.int16)

    def band_matrix(chunk):
        at = pl.ds(pl.multiple_of(chunk * LANES, LANES), LANES)
        offsets = jnp.broadcast_to(offset_ref[:, at], (16, LANES)).astype(jnp.int16)
        distance = delta - jnp.concatenate([offsets] * (2 * LANES // 16), 0)
        weights = kernel_ref[:, at]
        banded = jnp.zeros(window, jnp.bfloat16)
        for tap in range(weights.shape[0]):
            weight = jnp.broadcast_to(weights[tap : tap + 1], (16, LANES)).astype(jnp.bfloat16)
            weight = jnp.concatenate([weight] * (2 * LANES // 16), 0)
            banded = jnp.where(distance == jnp.int16(tap), weight, banded)
        b_ref[chunk] = banded

    def range_group(first):
        for apart in range(rwidth // LANES):
            count = GROUP - apart if groups == 1 else GROUP
            if apart < GROUP:
                band_matrix(first + apart)
            if count <= 0:
                continue
            at = slice(LANES * apart, LANES * (apart + 1))
            zr, zi, zn = zr_ref[:, at], zi_ref[:, at], zn_ref[:, at]
            weights = jnp.concatenate(
                [jnp.concatenate([zr, zi], 1), jnp.concatenate([zn, zr], 1)], 0
            )
            start = pl.multiple_of((first + apart) * rows, 16)
            product = jnp.dot(
                x_ref[pl.ds(start, count * rows), :],
                weights,
                preferred_element_type=jnp.float32,
            )
            if apart == 0:
                sum_ref[...] = product
            else:
                sum_ref[0 : count * rows, :] += product
        start = pl.multiple_of((first + 1) * rows, 16)
        f_ref[pl.ds(start, GROUP * rows), :] = sum_ref[...].astype(jnp.bfloat16)

    f_ref[0:rows, :] = jnp.zeros((rows, 2 * LANES), jnp.bfloat16)
    f_ref[(chunks + 1) * rows :, :] = jnp.zeros((rows, 2 * LANES), jnp.bfloat16)
    each_group(range_group)

    left = iota((rows, LANES), 1) < LANES // 2

    def migrate_group(first):
        ahead = list(range(1, GROUP, 2)) + list(range(2, GROUP + 1, 2))
        chunk_at = [lax.rem(lax.div(me, 2) + first + step, chunks) for step in ahead]

        def migrated(chunk):
            start = pl.multiple_of(chunk * rows, 16)
            before = f_ref[pl.ds(start, rows), :]
            here = f_ref[pl.ds(pl.multiple_of(start + rows, 16), rows), :]
            after = f_ref[pl.ds(pl.multiple_of(start + 2 * rows, 16), rows), :]
            both = []
            for part in (slice(0, LANES), slice(LANES, 2 * LANES)):
                around = jnp.where(left, before[:, part], after[:, part])
                both.append(jnp.concatenate([here[:, part], around], 1))
            moved = jnp.dot(
                jnp.concatenate(both, 0), b_ref[chunk], preferred_element_type=jnp.float32
            )
            real_part, imag_part = moved[:rows], moved[rows:]
            even = jnp.where(left, real_part, pltpu.roll(imag_part, LANES // 2, 1))
            odd = jnp.where(left, pltpu.roll(real_part, LANES // 2, 1), imag_part)
            return even.astype(jnp.bfloat16), odd.astype(jnp.bfloat16)

        later = [migrated(chunk) for chunk in chunk_at[:BATCH]]
        for at in range(0, GROUP, BATCH):
            now = later
            later = [migrated(chunk) for chunk in chunk_at[at + BATCH : at + 2 * BATCH]]
            batch = list(enumerate(chunk_at))[at : at + BATCH]
            for (j, chunk), pair in zip(batch, now):
                for half in range(2):
                    send_ref[2 * chunk + half] = pair[half]
            if groups == 1 and at == 0:
                pl.semaphore_wait(barrier, devices - 1)
            for j, chunk in batch:
                for half in range(2):
                    send(2 * chunk + half, groups > 1 or j == GROUP - 1)

    def send(other, own_possible):
        def go():
            pltpu.make_async_remote_copy(
                src_ref=send_ref.at[other],
                dst_ref=recv_ref.at[me],
                send_sem=send_sem,
                recv_sem=recv_sems.at[lax.div(me, sources)],
                device_id=place(other),
                device_id_type=MESH,
            ).start()

        if own_possible:
            pl.when(other != me)(go)
        else:
            go()

    if groups > 1:
        pl.semaphore_wait(barrier, devices - 1)
    each_group(migrate_group)
    own_copy = pltpu.make_async_copy(
        send_ref.at[me], recv_ref.at[me], recv_sems.at[lax.div(me, sources)]
    )
    own_copy.start()

    for copy in later_copies:
        copy.wait()
    for part in range(2):
        for start, moved_rows in shifted_rows(ataps_ref[part : part + 1, :], awidth, 8, 1):
            at = LANES * part + start
            za_ref[at : at + 16, :] = moved_rows

    base = (me - 1) * patches
    slot = iota((3 * patches, patches), 0) + base
    spread = jnp.zeros((3 * patches, patches), jnp.float32)
    for over in range(list_ref.shape[0]):
        spread += jnp.where(
            list_ref[over : over + 1, :] == slot, frac_ref[over : over + 1, :], 0.0
        )

    square = (LANES, LANES)
    column = iota(square, 1)
    parts_beside = (iota(square, 0) == LANES // 2 * (column % 2) + column // 2)
    parts_beside = parts_beside.astype(jnp.float32).astype(jnp.bfloat16)
    sign = jnp.where(iota(square, 1) < LANES // 2, -1.0, 1.0)

    for block in range(blocks):
        at = pl.ds(sources * block, sources)
        pltpu.make_async_copy(recv_ref.at[at], recv_ref.at[at], recv_sems.at[block]).wait()
        columns = recv_ref[sources * block : sources * (block + 1)].reshape(LANES, LANES)
        for apart in range(min(block + 1, awidth // LANES)):
            product = jnp.dot(
                za_ref[:, LANES * apart : LANES * (apart + 1)],
                columns,
                preferred_element_type=jnp.float32,
            )
            if apart == 0:
                focus_sum_ref[block] = product
            else:
                focus_sum_ref[block - apart] += product

    left_half = iota((LANES // 8, LANES), 1) < LANES // 2
    for block in range(blocks):
        product = focus_sum_ref[block]
        focus = product[:LANES] + sign * pltpu.roll(product[LANES:], LANES // 2, 1)
        focus_ref[LANES * block : LANES * (block + 1), :] = focus.astype(jnp.bfloat16)
        power = (focus * focus).reshape(2, LOOKS, LANES // 8, LANES)
        summed = []
        for half in range(2):
            total = power[half, 0]
            for look in range(1, LOOKS):
                total += power[half, look]
            summed.append(total + pltpu.roll(total, LANES // 2, 1))
        looked_ref[LANES // 8 * block : LANES // 8 * (block + 1), :] = jnp.where(
            left_half, summed[0], summed[1]
        ) * (1.0 / LOOKS)
    stride = LOOKS * PROWS // 8
    pieces = [looked_ref[pl.ds(piece, patches, stride=stride), :] for piece in range(stride)]
    looked = jnp.concatenate(pieces, 1)

    def tile_sums(first):
        weights = spread[first : first + patches]
        total = weights[:, 0:1] * looked[0:1, :]
        for patch in range(1, patches):
            total += weights[:, patch : patch + 1] * looked[patch : patch + 1, :]
        return total

    half_tile = looked.shape[1] // 2

    def packed(total):
        halves = [total[:, :half_tile], total[:, half_tile:]]
        return jnp.concatenate(halves, 0).astype(jnp.bfloat16)

    def unpacked(ref):
        total = ref[...].astype(jnp.float32)
        return jnp.concatenate([total[:patches], total[patches:]], 1)

    low_ref[...] = packed(tile_sums(0))
    high_ref[...] = packed(tile_sums(2 * patches))

    def low_copy():
        return pltpu.make_async_remote_copy(
            src_ref=low_ref,
            dst_ref=from_next_ref,
            send_sem=low_send_sem,
            recv_sem=low_recv_sem,
            device_id=place(jnp.maximum(me - 1, 0)),
            device_id_type=MESH,
        )

    def high_copy():
        return pltpu.make_async_remote_copy(
            src_ref=high_ref,
            dst_ref=from_prev_ref,
            send_sem=high_send_sem,
            recv_sem=high_recv_sem,
            device_id=place(jnp.minimum(me + 1, devices - 1)),
            device_id_type=MESH,
        )

    @pl.when(me > 0)
    def _():
        low_copy().start()

    @pl.when(me < devices - 1)
    def _():
        high_copy().start()

    tiles_ref[...] = tile_sums(patches)
    row = iota(square, 0)
    in_order = (column == row % 8 * (LANES // 8) + row // 8).astype(jnp.float32)
    in_order = in_order.astype(jnp.bfloat16)
    for block in range(blocks):
        at = slice(LANES * block, LANES * (block + 1))
        ordered = jnp.dot(in_order, focus_ref[at, :], preferred_element_type=jnp.float32)
        focused_ref[at, :] = jnp.dot(
            ordered.astype(jnp.bfloat16), parts_beside, preferred_element_type=jnp.float32
        ).astype(jnp.bfloat16)
    others = pl.ds(0, devices - 1)
    pltpu.make_async_copy(send_ref.at[others], send_ref.at[others], send_sem).wait()

    @pl.when(me < devices - 1)
    def _():
        low_copy().wait_recv()
        tiles_ref[...] += unpacked(from_next_ref)

    @pl.when(me > 0)
    def _():
        high_copy().wait_recv()
        tiles_ref[...] += unpacked(from_prev_ref)

    @pl.when(me > 0)
    def _():
        low_copy().wait_send()

    @pl.when(me < devices - 1)
    def _():
        high_copy().wait_send()


def body(
    raw_echoes, range_taps, mig_offset, interp_band, interp_table, azimuth_taps, geo_list, geo_frac
):
    across = lax.axis_size("range")
    devices = lax.axis_size("pulse") * across
    rows, breadth = raw_echoes.shape
    pulses = rows * devices
    bins = breadth // 2
    chunks = bins // LANES
    patches = geo_list.shape[1]
    tile = PROWS * (bins // devices)
    rwidth = min(bins, range_taps.shape[0] + LANES)
    awidth = min(pulses, azimuth_taps.shape[0] + LANES)
    spare = 0 if chunks == GROUP else rwidth // LANES
    whole = pl.BlockSpec(memory_space=pltpu.VMEM)
    operands = (
        raw_echoes,
        range_taps.T,
        mig_offset.reshape(1, bins),
        interp_band.reshape(1, bins),
        interp_table.T,
        azimuth_taps.T,
        geo_list[0].T,
        geo_frac[0].T,
    )
    scratch = [pltpu.VMEM(operand.shape, operand.dtype) for operand in operands] + [
        pltpu.VMEM((LANES, rwidth), jnp.bfloat16),
        pltpu.VMEM((LANES, rwidth), jnp.bfloat16),
        pltpu.VMEM((LANES, rwidth), jnp.bfloat16),
        pltpu.VMEM((2 * LANES, awidth), jnp.bfloat16),
        pltpu.VMEM(((chunks + spare) * rows, 2 * LANES), jnp.bfloat16),
        pltpu.VMEM((GROUP * rows, 2 * LANES), jnp.float32),
        pltpu.VMEM(((chunks + 2) * rows, 2 * LANES), jnp.bfloat16),
        pltpu.VMEM((interp_table.shape[1], bins), jnp.float32),
        pltpu.VMEM((chunks, 2 * LANES, LANES), jnp.bfloat16),
        pltpu.VMEM((devices, rows, LANES), jnp.bfloat16),
        pltpu.VMEM((devices, rows, LANES), jnp.bfloat16),
        pltpu.VMEM((pulses, LANES), jnp.bfloat16),
        pltpu.VMEM((pulses // LANES, 2 * LANES, LANES), jnp.float32),
        pltpu.VMEM((pulses // 8, LANES), jnp.float32),
        pltpu.VMEM((2 * patches, tile // 2), jnp.bfloat16),
        pltpu.VMEM((2 * patches, tile // 2), jnp.bfloat16),
        pltpu.VMEM((2 * patches, tile // 2), jnp.bfloat16),
        pltpu.VMEM((2 * patches, tile // 2), jnp.bfloat16),
    ] + [
        pltpu.SemaphoreType.DMA((8,)),
        pltpu.SemaphoreType.DMA,
        pltpu.SemaphoreType.DMA((pulses // LANES,)),
    ] + [pltpu.SemaphoreType.DMA] * 4
    shapes = (
        jax.ShapeDtypeStruct((pulses, breadth // devices), jnp.bfloat16),
        jax.ShapeDtypeStruct((patches, tile), jnp.float32),
    )
    outside = pl.BlockSpec(memory_space=pltpu.HBM)
    return pl.pallas_call(
        functools.partial(kernel, devices, across),
        out_shape=shapes,
        in_specs=[outside] * 8,
        out_specs=(whole, whole),
        scratch_shapes=scratch,
        compiler_params=pltpu.CompilerParams(
            collective_id=0, has_side_effects=True, vmem_limit_bytes=40 * 2**20
        ),
    )(*[pltpu.with_memory_space_constraint(operand, pltpu.HBM) for operand in operands])


def solution(mesh):
    placed = (
        P(("pulse", "range"), None),
        P(),
        P(),
        P(),
        P(),
        P(),
        P(("pulse", "range"), None, None),
        P(("pulse", "range"), None, None),
    )
    return jax.shard_map(
        body,
        mesh=mesh,
        in_specs=placed,
        out_specs=(P(None, ("pulse", "range")), P(("pulse", "range"), None)),
        check_vma=False,
    )
```

```python
import functools

import jax
import jax.numpy as jnp
from jax import lax
from jax.experimental import pallas as pl
from jax.experimental.pallas import tpu as pltpu
from jax.sharding import PartitionSpec as P

LOOKS = 4
PROWS = 16
LANES = 128
GROUP = 16
BATCH = 16
MESH = pl.DeviceIdType.MESH


def iota(shape, dim):
    return lax.broadcasted_iota(jnp.int32, shape, dim)


def shifted_rows(taps, width, stride, step):
    have = min(width, taps.shape[1])
    line = taps[:, :have].astype(jnp.float32)
    if have < width:
        line = jnp.concatenate([line, jnp.zeros((1, width - have), jnp.float32)], 1)
    eight = jnp.broadcast_to(line, (8, width))
    row = iota((8, width), 0)
    for bit in (1, 2, 4):
        eight = jnp.where((row & bit) != 0, pltpu.roll(eight, bit * stride, 1), eight)
    both = jnp.concatenate([eight, pltpu.roll(eight, 8 * stride, 1)], 0).astype(jnp.bfloat16)
    tile = (16, LANES)
    for part in range(LANES // 16):
        moved = both if part == 0 else pltpu.roll(both, step * part, 1)
        keep = iota(tile, 1) >= iota(tile, 0) * stride + step * part
        first = jnp.where(keep, moved[:, :LANES], jnp.zeros(tile, jnp.bfloat16))
        yield 16 * part, jnp.concatenate([first, moved[:, LANES:]], 1)


def kernel(
    devices,
    across,
    raw_in,
    rtaps_in,
    offset_in,
    band_in,
    table_in,
    ataps_in,
    list_in,
    frac_in,
    focused_ref,
    tiles_ref,
    raw_ref,
    rtaps_ref,
    offset_ref,
    band_ref,
    table_ref,
    ataps_ref,
    list_ref,
    frac_ref,
    zr_ref,
    zi_ref,
    zn_ref,
    za_ref,
    x_ref,
    sum_ref,
    f_ref,
    kernel_ref,
    b_ref,
    send_ref,
    recv_ref,
    focus_ref,
    focus_sum_ref,
    looked_ref,
    low_ref,
    high_ref,
    from_next_ref,
    from_prev_ref,
    in_sems,
    send_sem,
    recv_sems,
    low_send_sem,
    high_send_sem,
    low_recv_sem,
    high_recv_sem,
):
    pulse_at, range_at = lax.axis_index("pulse"), lax.axis_index("range")
    me = pulse_at * across + range_at
    rows, breadth = raw_ref.shape
    chunks = breadth // (2 * LANES)
    groups = chunks // GROUP
    pulses = devices * rows
    patches = list_ref.shape[1]
    sources = LANES // rows
    blocks = pulses // LANES
    rwidth = zr_ref.shape[1]
    awidth = za_ref.shape[1]

    rtaps_copy, raw_copy, offset_copy, band_copy, table_copy, ataps_copy, list_copy, frac_copy = [
        pltpu.make_async_copy(outside, inside, in_sems.at[at])
        for at, (outside, inside) in enumerate(
            (
                (rtaps_in, rtaps_ref),
                (raw_in, raw_ref),
                (offset_in, offset_ref),
                (band_in, band_ref),
                (table_in, table_ref),
                (ataps_in, ataps_ref),
                (list_in, list_ref),
                (frac_in, frac_ref),
            )
        )
    ]
    first_copies = (rtaps_copy, offset_copy, band_copy, table_copy, raw_copy)
    later_copies = (ataps_copy, list_copy, frac_copy)
    rtaps_copy.start()
    raw_copy.start()

    def place(index):
        return (lax.div(index, across), lax.rem(index, across))

    barrier = pltpu.get_barrier_semaphore()

    def greet(distance, carry):
        other = lax.rem(me + distance, devices)
        pl.semaphore_signal(barrier, inc=1, device_id=place(other), device_id_type=MESH)
        return carry

    if groups == 1:
        for distance in range(1, devices):
            greet(distance, 0)
    else:
        lax.fori_loop(1, devices, greet, 0)
    for copy in (offset_copy, band_copy, table_copy) + later_copies:
        copy.start()

    def each_group(body):
        if groups == 1:
            body(0)
        else:
            lax.fori_loop(0, groups, lambda g, c: (body(g * GROUP), c)[1], 0)

    rtaps_copy.wait()

    for start, real_rows in shifted_rows(rtaps_ref[0:1, :], rwidth, 1, 16):
        zr_ref[start : start + 16, :] = real_rows
    for start, imag_rows in shifted_rows(rtaps_ref[1:2, :], rwidth, 1, 16):
        zi_ref[start : start + 16, :] = imag_rows
        zn_ref[start : start + 16, :] = -imag_rows

    for copy in first_copies[1:]:
        copy.wait()

    side = (2 * LANES, 2 * LANES)
    column = iota(side, 1)
    source = 2 * (LANES - 1 - (column % LANES)) + column // LANES
    parts_apart = (iota(side, 0) == source).astype(jnp.float32).astype(jnp.bfloat16)
    lines = jnp.concatenate(
        [raw_ref[:, 2 * LANES * j : 2 * LANES * (j + 1)] for j in range(chunks)], 0
    )
    x_ref[0 : chunks * rows, :] = jnp.dot(
        lines, parts_apart, preferred_element_type=jnp.float32
    ).astype(jnp.bfloat16)
    spare = x_ref.shape[0] - chunks * rows
    if spare:
        x_ref[chunks * rows :, :] = jnp.zeros((spare, 2 * LANES), jnp.bfloat16)

    bands, bins = table_ref.shape[1], chunks * LANES
    onehot = (iota((bands, bins), 0) == band_ref[...]).astype(jnp.float32).astype(jnp.bfloat16)
    kernel_ref[...] = jnp.dot(table_ref[...], onehot, preferred_element_type=jnp.float32)
    window = (2 * LANES, LANES)
    lane = iota(window, 0) % LANES
    shift = jnp.where(lane < LANES // 2, -LANES, LANES)
    bin_of = LANES - 1 - lane + jnp.where(iota(window, 0) < LANES, 0, shift)
    delta = (bin_of - iota(window, 1) + 3).astype(jnp.int16)

    def band_matrix(chunk):
        at = pl.ds(pl.multiple_of(chunk * LANES, LANES), LANES)
        offsets = jnp.broadcast_to(offset_ref[:, at], (16, LANES)).astype(jnp.int16)
        distance = delta - jnp.concatenate([offsets] * (2 * LANES // 16), 0)
        weights = kernel_ref[:, at]
        banded = jnp.zeros(window, jnp.bfloat16)
        for tap in range(weights.shape[0]):
            weight = jnp.broadcast_to(weights[tap : tap + 1], (16, LANES)).astype(jnp.bfloat16)
            weight = jnp.concatenate([weight] * (2 * LANES // 16), 0)
            banded = jnp.where(distance == jnp.int16(tap), weight, banded)
        b_ref[chunk] = banded

    def range_group(first):
        for apart in range(rwidth // LANES):
            count = GROUP - apart if groups == 1 else GROUP
            if apart < GROUP:
                band_matrix(first + apart)
            if count <= 0:
                continue
            at = slice(LANES * apart, LANES * (apart + 1))
            zr, zi, zn = zr_ref[:, at], zi_ref[:, at], zn_ref[:, at]
            weights = jnp.concatenate(
                [jnp.concatenate([zr, zi], 1), jnp.concatenate([zn, zr], 1)], 0
            )
            start = pl.multiple_of((first + apart) * rows, 16)
            product = jnp.dot(
                x_ref[pl.ds(start, count * rows), :],
                weights,
                preferred_element_type=jnp.float32,
            )
            if apart == 0:
                sum_ref[...] = product
            else:
                sum_ref[0 : count * rows, :] += product
        start = pl.multiple_of((first + 1) * rows, 16)
        f_ref[pl.ds(start, GROUP * rows), :] = sum_ref[...].astype(jnp.bfloat16)

    f_ref[0:rows, :] = jnp.zeros((rows, 2 * LANES), jnp.bfloat16)
    f_ref[(chunks + 1) * rows :, :] = jnp.zeros((rows, 2 * LANES), jnp.bfloat16)
    each_group(range_group)

    left = iota((rows, LANES), 1) < LANES // 2

    def migrate_group(first):
        ahead = list(range(1, GROUP, 2)) + list(range(2, GROUP + 1, 2))
        chunk_at = [lax.rem(lax.div(me, 2) + first + step, chunks) for step in ahead]

        def migrated(chunk):
            start = pl.multiple_of(chunk * rows, 16)
            before = f_ref[pl.ds(start, rows), :]
            here = f_ref[pl.ds(pl.multiple_of(start + rows, 16), rows), :]
            after = f_ref[pl.ds(pl.multiple_of(start + 2 * rows, 16), rows), :]
            both = []
            for part in (slice(0, LANES), slice(LANES, 2 * LANES)):
                around = jnp.where(left, before[:, part], after[:, part])
                both.append(jnp.concatenate([here[:, part], around], 1))
            moved = jnp.dot(
                jnp.concatenate(both, 0), b_ref[chunk], preferred_element_type=jnp.float32
            )
            real_part, imag_part = moved[:rows], moved[rows:]
            even = jnp.where(left, real_part, pltpu.roll(imag_part, LANES // 2, 1))
            odd = jnp.where(left, pltpu.roll(real_part, LANES // 2, 1), imag_part)
            return even.astype(jnp.bfloat16), odd.astype(jnp.bfloat16)

        later = [migrated(chunk) for chunk in chunk_at[:BATCH]]
        for at in range(0, GROUP, BATCH):
            now = later
            later = [migrated(chunk) for chunk in chunk_at[at + BATCH : at + 2 * BATCH]]
            batch = list(enumerate(chunk_at))[at : at + BATCH]
            for (j, chunk), pair in zip(batch, now):
                for half in range(2):
                    send_ref[2 * chunk + half] = pair[half]
            if groups == 1 and at == 0:
                pl.semaphore_wait(barrier, devices - 1)
            for j, chunk in batch:
                for half in range(2):
                    send(2 * chunk + half, groups > 1 or j == GROUP - 1)

    def send(other, own_possible):
        def go():
            pltpu.make_async_remote_copy(
                src_ref=send_ref.at[other],
                dst_ref=recv_ref.at[me],
                send_sem=send_sem,
                recv_sem=recv_sems.at[lax.div(me, sources)],
                device_id=place(other),
                device_id_type=MESH,
            ).start()

        if own_possible:
            pl.when(other != me)(go)
        else:
            go()

    if groups > 1:
        pl.semaphore_wait(barrier, devices - 1)
    each_group(migrate_group)
    own_copy = pltpu.make_async_copy(
        send_ref.at[me], recv_ref.at[me], recv_sems.at[lax.div(me, sources)]
    )
    own_copy.start()

    for copy in later_copies:
        copy.wait()
    for part in range(2):
        for start, moved_rows in shifted_rows(ataps_ref[part : part + 1, :], awidth, 8, 1):
            at = LANES * part + start
            za_ref[at : at + 16, :] = moved_rows

    base = (me - 1) * patches
    slot = iota((3 * patches, patches), 0) + base
    spread = jnp.zeros((3 * patches, patches), jnp.float32)
    for over in range(list_ref.shape[0]):
        spread += jnp.where(
            list_ref[over : over + 1, :] == slot, frac_ref[over : over + 1, :], 0.0
        )

    square = (LANES, LANES)
    column = iota(square, 1)
    parts_beside = (iota(square, 0) == LANES // 2 * (column % 2) + column // 2)
    parts_beside = parts_beside.astype(jnp.float32).astype(jnp.bfloat16)
    sign = jnp.where(iota(square, 1) < LANES // 2, -1.0, 1.0)

    for block in range(blocks):
        at = pl.ds(sources * block, sources)
        pltpu.make_async_copy(recv_ref.at[at], recv_ref.at[at], recv_sems.at[block]).wait()
        columns = recv_ref[sources * block : sources * (block + 1)].reshape(LANES, LANES)
        for apart in range(min(block + 1, awidth // LANES)):
            product = jnp.dot(
                za_ref[:, LANES * apart : LANES * (apart + 1)],
                columns,
                preferred_element_type=jnp.float32,
            )
            if apart == 0:
                focus_sum_ref[block] = product
            else:
                focus_sum_ref[block - apart] += product

    left_half = iota((LANES // 8, LANES), 1) < LANES // 2
    for block in range(blocks):
        product = focus_sum_ref[block]
        focus = product[:LANES] + sign * pltpu.roll(product[LANES:], LANES // 2, 1)
        focus_ref[LANES * block : LANES * (block + 1), :] = focus.astype(jnp.bfloat16)
        power = (focus * focus).reshape(2, LOOKS, LANES // 8, LANES)
        summed = []
        for half in range(2):
            total = power[half, 0]
            for look in range(1, LOOKS):
                total += power[half, look]
            summed.append(total + pltpu.roll(total, LANES // 2, 1))
        looked_ref[LANES // 8 * block : LANES // 8 * (block + 1), :] = jnp.where(
            left_half, summed[0], summed[1]
        ) * (1.0 / LOOKS)
    stride = LOOKS * PROWS // 8
    pieces = [looked_ref[pl.ds(piece, patches, stride=stride), :] for piece in range(stride)]
    looked = jnp.concatenate(pieces, 1)

    def tile_sums(first):
        weights = spread[first : first + patches]
        total = weights[:, 0:1] * looked[0:1, :]
        for patch in range(1, patches):
            total += weights[:, patch : patch + 1] * looked[patch : patch + 1, :]
        return total

    half_tile = looked.shape[1] // 2

    def packed(total):
        halves = [total[:, :half_tile], total[:, half_tile:]]
        return jnp.concatenate(halves, 0).astype(jnp.bfloat16)

    def unpacked(ref):
        total = ref[...].astype(jnp.float32)
        return jnp.concatenate([total[:patches], total[patches:]], 1)

    low_ref[...] = packed(tile_sums(0))
    high_ref[...] = packed(tile_sums(2 * patches))

    def low_copy():
        return pltpu.make_async_remote_copy(
            src_ref=low_ref,
            dst_ref=from_next_ref,
            send_sem=low_send_sem,
            recv_sem=low_recv_sem,
            device_id=place(jnp.maximum(me - 1, 0)),
            device_id_type=MESH,
        )

    def high_copy():
        return pltpu.make_async_remote_copy(
            src_ref=high_ref,
            dst_ref=from_prev_ref,
            send_sem=high_send_sem,
            recv_sem=high_recv_sem,
            device_id=place(jnp.minimum(me + 1, devices - 1)),
            device_id_type=MESH,
        )

    @pl.when(me > 0)
    def _():
        low_copy().start()

    @pl.when(me < devices - 1)
    def _():
        high_copy().start()

    tiles_ref[...] = tile_sums(patches)
    row = iota(square, 0)
    in_order = (column == row % 8 * (LANES // 8) + row // 8).astype(jnp.float32)
    in_order = in_order.astype(jnp.bfloat16)
    for block in range(blocks):
        at = slice(LANES * block, LANES * (block + 1))
        ordered = jnp.dot(in_order, focus_ref[at, :], preferred_element_type=jnp.float32)
        focused_ref[at, :] = jnp.dot(
            ordered.astype(jnp.bfloat16), parts_beside, preferred_element_type=jnp.float32
        ).astype(jnp.bfloat16)
    others = pl.ds(0, devices - 1)
    pltpu.make_async_copy(send_ref.at[others], send_ref.at[others], send_sem).wait()

    @pl.when(me < devices - 1)
    def _():
        low_copy().wait_recv()
        tiles_ref[...] += unpacked(from_next_ref)

    @pl.when(me > 0)
    def _():
        high_copy().wait_recv()
        tiles_ref[...] += unpacked(from_prev_ref)

    @pl.when(me > 0)
    def _():
        low_copy().wait_send()

    @pl.when(me < devices - 1)
    def _():
        high_copy().wait_send()


def hand_out(focused_ref, tiles_ref, focused_out, tiles_out, sems):
    copies = (
        pltpu.make_async_copy(focused_ref, focused_out, sems.at[0]),
        pltpu.make_async_copy(tiles_ref, tiles_out, sems.at[1]),
    )
    for copy in copies:
        copy.start()
    for copy in copies:
        copy.wait()


def body(
    raw_echoes, range_taps, mig_offset, interp_band, interp_table, azimuth_taps, geo_list, geo_frac
):
    across = lax.axis_size("range")
    devices = lax.axis_size("pulse") * across
    rows, breadth = raw_echoes.shape
    pulses = rows * devices
    bins = breadth // 2
    chunks = bins // LANES
    patches = geo_list.shape[1]
    tile = PROWS * (bins // devices)
    rwidth = min(bins, range_taps.shape[0] + LANES)
    awidth = min(pulses, azimuth_taps.shape[0] + LANES)
    spare = 0 if chunks == GROUP else rwidth // LANES
    whole = pl.BlockSpec(memory_space=pltpu.VMEM)
    operands = (
        raw_echoes,
        range_taps.T,
        mig_offset.reshape(1, bins),
        interp_band.reshape(1, bins),
        interp_table.T,
        azimuth_taps.T,
        geo_list[0].T,
        geo_frac[0].T,
    )
    scratch = [pltpu.VMEM(operand.shape, operand.dtype) for operand in operands] + [
        pltpu.VMEM((LANES, rwidth), jnp.bfloat16),
        pltpu.VMEM((LANES, rwidth), jnp.bfloat16),
        pltpu.VMEM((LANES, rwidth), jnp.bfloat16),
        pltpu.VMEM((2 * LANES, awidth), jnp.bfloat16),
        pltpu.VMEM(((chunks + spare) * rows, 2 * LANES), jnp.bfloat16),
        pltpu.VMEM((GROUP * rows, 2 * LANES), jnp.float32),
        pltpu.VMEM(((chunks + 2) * rows, 2 * LANES), jnp.bfloat16),
        pltpu.VMEM((interp_table.shape[1], bins), jnp.float32),
        pltpu.VMEM((chunks, 2 * LANES, LANES), jnp.bfloat16),
        pltpu.VMEM((devices, rows, LANES), jnp.bfloat16),
        pltpu.VMEM((devices, rows, LANES), jnp.bfloat16),
        pltpu.VMEM((pulses, LANES), jnp.bfloat16),
        pltpu.VMEM((pulses // LANES, 2 * LANES, LANES), jnp.float32),
        pltpu.VMEM((pulses // 8, LANES), jnp.float32),
        pltpu.VMEM((2 * patches, tile // 2), jnp.bfloat16),
        pltpu.VMEM((2 * patches, tile // 2), jnp.bfloat16),
        pltpu.VMEM((2 * patches, tile // 2), jnp.bfloat16),
        pltpu.VMEM((2 * patches, tile // 2), jnp.bfloat16),
    ] + [
        pltpu.SemaphoreType.DMA((8,)),
        pltpu.SemaphoreType.DMA,
        pltpu.SemaphoreType.DMA((pulses // LANES,)),
    ] + [pltpu.SemaphoreType.DMA] * 4
    shapes = (
        jax.ShapeDtypeStruct((pulses, breadth // devices), jnp.bfloat16),
        jax.ShapeDtypeStruct((patches, tile), jnp.float32),
    )
    outside = pl.BlockSpec(memory_space=pltpu.HBM)
    results = pl.pallas_call(
        functools.partial(kernel, devices, across),
        out_shape=shapes,
        in_specs=[outside] * 8,
        out_specs=(whole, whole),
        scratch_shapes=scratch,
        compiler_params=pltpu.CompilerParams(
            collective_id=0, has_side_effects=True, vmem_limit_bytes=40 * 2**20
        ),
    )(*[pltpu.with_memory_space_constraint(operand, pltpu.HBM) for operand in operands])
    return pl.pallas_call(
        hand_out,
        out_shape=shapes,
        in_specs=[whole] * 2,
        out_specs=(outside, outside),
        scratch_shapes=[pltpu.SemaphoreType.DMA((2,))],
    )(*[pltpu.with_memory_space_constraint(result, pltpu.VMEM) for result in results])


def solution(mesh):
    placed = (
        P(("pulse", "range"), None),
        P(),
        P(),
        P(),
        P(),
        P(),
        P(("pulse", "range"), None, None),
        P(("pulse", "range"), None, None),
    )
    return jax.shard_map(
        body,
        mesh=mesh,
        in_specs=placed,
        out_specs=(P(None, ("pulse", "range")), P(("pulse", "range"), None)),
        check_vma=False,
    )
```

```python
import functools

import jax
import jax.numpy as jnp
from jax import lax
from jax.experimental import pallas as pl
from jax.experimental.pallas import tpu as pltpu
from jax.sharding import PartitionSpec as P

LOOKS = 4
PROWS = 16
LANES = 128
GROUP = 16
BATCH = 16
MESH = pl.DeviceIdType.MESH


def iota(shape, dim):
    return lax.broadcasted_iota(jnp.int32, shape, dim)


def shifted_rows(taps, width, stride, step):
    have = min(width, taps.shape[1])
    line = taps[:, :have].astype(jnp.float32)
    if have < width:
        line = jnp.concatenate([line, jnp.zeros((1, width - have), jnp.float32)], 1)
    eight = jnp.broadcast_to(line, (8, width))
    row = iota((8, width), 0)
    for bit in (1, 2, 4):
        eight = jnp.where((row & bit) != 0, pltpu.roll(eight, bit * stride, 1), eight)
    both = jnp.concatenate([eight, pltpu.roll(eight, 8 * stride, 1)], 0).astype(jnp.bfloat16)
    tile = (16, LANES)
    for part in range(LANES // 16):
        moved = both if part == 0 else pltpu.roll(both, step * part, 1)
        keep = iota(tile, 1) >= iota(tile, 0) * stride + step * part
        first = jnp.where(keep, moved[:, :LANES], jnp.zeros(tile, jnp.bfloat16))
        yield 16 * part, jnp.concatenate([first, moved[:, LANES:]], 1)


def kernel(
    devices,
    across,
    raw_in,
    rtaps_in,
    offset_in,
    band_in,
    table_in,
    ataps_in,
    list_in,
    frac_in,
    focused_ref,
    tiles_ref,
    raw_ref,
    rtaps_ref,
    offset_ref,
    band_ref,
    table_ref,
    ataps_ref,
    list_ref,
    frac_ref,
    zr_ref,
    zi_ref,
    zn_ref,
    za_ref,
    x_ref,
    sum_ref,
    f_ref,
    kernel_ref,
    b_ref,
    send_ref,
    recv_ref,
    focus_ref,
    focus_sum_ref,
    looked_ref,
    low_ref,
    high_ref,
    from_next_ref,
    from_prev_ref,
    in_sems,
    send_sem,
    recv_sems,
    low_send_sem,
    high_send_sem,
    low_recv_sem,
    high_recv_sem,
):
    pulse_at, range_at = lax.axis_index("pulse"), lax.axis_index("range")
    me = pulse_at * across + range_at
    rows, breadth = raw_ref.shape
    chunks = breadth // (2 * LANES)
    groups = chunks // GROUP
    pulses = devices * rows
    patches = list_ref.shape[1]
    sources = LANES // rows
    blocks = pulses // LANES
    rwidth = zr_ref.shape[1]
    awidth = za_ref.shape[1]

    rtaps_copy, raw_copy, offset_copy, band_copy, table_copy, ataps_copy, list_copy, frac_copy = [
        pltpu.make_async_copy(outside, inside, in_sems.at[at])
        for at, (outside, inside) in enumerate(
            (
                (rtaps_in, rtaps_ref),
                (raw_in, raw_ref),
                (offset_in, offset_ref),
                (band_in, band_ref),
                (table_in, table_ref),
                (ataps_in, ataps_ref),
                (list_in, list_ref),
                (frac_in, frac_ref),
            )
        )
    ]
    first_copies = (rtaps_copy, raw_copy, offset_copy, band_copy, table_copy)
    later_copies = (ataps_copy, list_copy, frac_copy)

    def place(index):
        return (lax.div(index, across), lax.rem(index, across))

    barrier = pltpu.get_barrier_semaphore()

    def greet(distance, carry):
        other = lax.rem(me + distance, devices)
        pl.semaphore_signal(barrier, inc=1, device_id=place(other), device_id_type=MESH)
        return carry

    if groups == 1:
        for distance in range(1, devices):
            greet(distance, 0)
    else:
        lax.fori_loop(1, devices, greet, 0)
    for copy in first_copies + later_copies:
        copy.start()

    def each_group(body):
        if groups == 1:
            body(0)
        else:
            lax.fori_loop(0, groups, lambda g, c: (body(g * GROUP), c)[1], 0)

    rtaps_copy.wait()

    for start, real_rows in shifted_rows(rtaps_ref[0:1, :], rwidth, 1, 16):
        zr_ref[start : start + 16, :] = real_rows
    for start, imag_rows in shifted_rows(rtaps_ref[1:2, :], rwidth, 1, 16):
        zi_ref[start : start + 16, :] = imag_rows
        zn_ref[start : start + 16, :] = -imag_rows

    for copy in first_copies[1:]:
        copy.wait()

    side = (2 * LANES, 2 * LANES)
    column = iota(side, 1)
    source = 2 * (LANES - 1 - (column % LANES)) + column // LANES
    parts_apart = (iota(side, 0) == source).astype(jnp.float32).astype(jnp.bfloat16)
    lines = jnp.concatenate(
        [raw_ref[:, 2 * LANES * j : 2 * LANES * (j + 1)] for j in range(chunks)], 0
    )
    x_ref[0 : chunks * rows, :] = jnp.dot(
        lines, parts_apart, preferred_element_type=jnp.float32
    ).astype(jnp.bfloat16)
    spare = x_ref.shape[0] - chunks * rows
    if spare:
        x_ref[chunks * rows :, :] = jnp.zeros((spare, 2 * LANES), jnp.bfloat16)

    bands, bins = table_ref.shape[1], chunks * LANES
    onehot = (iota((bands, bins), 0) == band_ref[...]).astype(jnp.float32).astype(jnp.bfloat16)
    kernel_ref[...] = jnp.dot(table_ref[...], onehot, preferred_element_type=jnp.float32)
    window = (2 * LANES, LANES)
    lane = iota(window, 0) % LANES
    shift = jnp.where(lane < LANES // 2, -LANES, LANES)
    bin_of = LANES - 1 - lane + jnp.where(iota(window, 0) < LANES, 0, shift)
    delta = (bin_of - iota(window, 1) + 3).astype(jnp.int16)

    def band_matrix(chunk):
        at = pl.ds(pl.multiple_of(chunk * LANES, LANES), LANES)
        offsets = jnp.broadcast_to(offset_ref[:, at], (16, LANES)).astype(jnp.int16)
        distance = delta - jnp.concatenate([offsets] * (2 * LANES // 16), 0)
        weights = kernel_ref[:, at]
        banded = jnp.zeros(window, jnp.bfloat16)
        for tap in range(weights.shape[0]):
            weight = jnp.broadcast_to(weights[tap : tap + 1], (16, LANES)).astype(jnp.bfloat16)
            weight = jnp.concatenate([weight] * (2 * LANES // 16), 0)
            banded = jnp.where(distance == jnp.int16(tap), weight, banded)
        b_ref[chunk] = banded

    def range_group(first):
        for apart in range(rwidth // LANES):
            count = GROUP - apart if groups == 1 else GROUP
            if apart < GROUP:
                band_matrix(first + apart)
            if count <= 0:
                continue
            at = slice(LANES * apart, LANES * (apart + 1))
            zr, zi, zn = zr_ref[:, at], zi_ref[:, at], zn_ref[:, at]
            weights = jnp.concatenate(
                [jnp.concatenate([zr, zi], 1), jnp.concatenate([zn, zr], 1)], 0
            )
            start = pl.multiple_of((first + apart) * rows, 16)
            product = jnp.dot(
                x_ref[pl.ds(start, count * rows), :],
                weights,
                preferred_element_type=jnp.float32,
            )
            if apart == 0:
                sum_ref[...] = product
            else:
                sum_ref[0 : count * rows, :] += product
        start = pl.multiple_of((first + 1) * rows, 16)
        f_ref[pl.ds(start, GROUP * rows), :] = sum_ref[...].astype(jnp.bfloat16)

    f_ref[0:rows, :] = jnp.zeros((rows, 2 * LANES), jnp.bfloat16)
    f_ref[(chunks + 1) * rows :, :] = jnp.zeros((rows, 2 * LANES), jnp.bfloat16)
    each_group(range_group)

    left = iota((rows, LANES), 1) < LANES // 2

    def migrate_group(first):
        ahead = list(range(1, GROUP, 2)) + list(range(2, GROUP + 1, 2))
        chunk_at = [lax.rem(lax.div(me, 2) + first + step, chunks) for step in ahead]

        def migrated(chunk):
            start = pl.multiple_of(chunk * rows, 16)
            before = f_ref[pl.ds(start, rows), :]
            here = f_ref[pl.ds(pl.multiple_of(start + rows, 16), rows), :]
            after = f_ref[pl.ds(pl.multiple_of(start + 2 * rows, 16), rows), :]
            both = []
            for part in (slice(0, LANES), slice(LANES, 2 * LANES)):
                around = jnp.where(left, before[:, part], after[:, part])
                both.append(jnp.concatenate([here[:, part], around], 1))
            moved = jnp.dot(
                jnp.concatenate(both, 0), b_ref[chunk], preferred_element_type=jnp.float32
            )
            real_part, imag_part = moved[:rows], moved[rows:]
            even = jnp.where(left, real_part, pltpu.roll(imag_part, LANES // 2, 1))
            odd = jnp.where(left, pltpu.roll(real_part, LANES // 2, 1), imag_part)
            return even.astype(jnp.bfloat16), odd.astype(jnp.bfloat16)

        later = [migrated(chunk) for chunk in chunk_at[:BATCH]]
        for at in range(0, GROUP, BATCH):
            now = later
            later = [migrated(chunk) for chunk in chunk_at[at + BATCH : at + 2 * BATCH]]
            batch = list(enumerate(chunk_at))[at : at + BATCH]
            for (j, chunk), pair in zip(batch, now):
                for half in range(2):
                    send_ref[2 * chunk + half] = pair[half]
            if groups == 1 and at == 0:
                pl.semaphore_wait(barrier, devices - 1)
            for j, chunk in batch:
                for half in range(2):
                    send(2 * chunk + half, groups > 1 or j == GROUP - 1)

    def send(other, own_possible):
        def go():
            pltpu.make_async_remote_copy(
                src_ref=send_ref.at[other],
                dst_ref=recv_ref.at[me],
                send_sem=send_sem,
                recv_sem=recv_sems.at[lax.div(me, sources)],
                device_id=place(other),
                device_id_type=MESH,
            ).start()

        if own_possible:
            pl.when(other != me)(go)
        else:
            go()

    if groups > 1:
        pl.semaphore_wait(barrier, devices - 1)
    each_group(migrate_group)
    own_copy = pltpu.make_async_copy(
        send_ref.at[me], recv_ref.at[me], recv_sems.at[lax.div(me, sources)]
    )
    own_copy.start()

    for copy in later_copies:
        copy.wait()
    for part in range(2):
        for start, moved_rows in shifted_rows(ataps_ref[part : part + 1, :], awidth, 8, 1):
            at = LANES * part + start
            za_ref[at : at + 16, :] = moved_rows

    base = (me - 1) * patches
    slot = iota((3 * patches, patches), 0) + base
    spread = jnp.zeros((3 * patches, patches), jnp.float32)
    for over in range(list_ref.shape[0]):
        spread += jnp.where(
            list_ref[over : over + 1, :] == slot, frac_ref[over : over + 1, :], 0.0
        )

    square = (LANES, LANES)
    column = iota(square, 1)
    parts_beside = (iota(square, 0) == LANES // 2 * (column % 2) + column // 2)
    parts_beside = parts_beside.astype(jnp.float32).astype(jnp.bfloat16)
    sign = jnp.where(iota(square, 1) < LANES // 2, -1.0, 1.0)

    for block in range(blocks):
        at = pl.ds(sources * block, sources)
        pltpu.make_async_copy(recv_ref.at[at], recv_ref.at[at], recv_sems.at[block]).wait()
        columns = recv_ref[sources * block : sources * (block + 1)].reshape(LANES, LANES)
        for apart in range(min(block + 1, awidth // LANES)):
            product = jnp.dot(
                za_ref[:, LANES * apart : LANES * (apart + 1)],
                columns,
                preferred_element_type=jnp.float32,
            )
            if apart == 0:
                focus_sum_ref[block] = product
            else:
                focus_sum_ref[block - apart] += product

    left_half = iota((LANES // 8, LANES), 1) < LANES // 2
    for block in range(blocks):
        product = focus_sum_ref[block]
        focus = product[:LANES] + sign * pltpu.roll(product[LANES:], LANES // 2, 1)
        focus_ref[LANES * block : LANES * (block + 1), :] = focus.astype(jnp.bfloat16)
        power = (focus * focus).reshape(2, LOOKS, LANES // 8, LANES)
        summed = []
        for half in range(2):
            total = power[half, 0]
            for look in range(1, LOOKS):
                total += power[half, look]
            summed.append(total + pltpu.roll(total, LANES // 2, 1))
        looked_ref[LANES // 8 * block : LANES // 8 * (block + 1), :] = jnp.where(
            left_half, summed[0], summed[1]
        ) * (1.0 / LOOKS)
    stride = LOOKS * PROWS // 8
    pieces = [looked_ref[pl.ds(piece, patches, stride=stride), :] for piece in range(stride)]
    looked = jnp.concatenate(pieces, 1)

    def tile_sums(first):
        weights = spread[first : first + patches]
        total = weights[:, 0:1] * looked[0:1, :]
        for patch in range(1, patches):
            total += weights[:, patch : patch + 1] * looked[patch : patch + 1, :]
        return total

    half_tile = looked.shape[1] // 2

    def packed(total):
        halves = [total[:, :half_tile], total[:, half_tile:]]
        return jnp.concatenate(halves, 0).astype(jnp.bfloat16)

    def unpacked(ref):
        total = ref[...].astype(jnp.float32)
        return jnp.concatenate([total[:patches], total[patches:]], 1)

    low_ref[...] = packed(tile_sums(0))

    def low_copy():
        return pltpu.make_async_remote_copy(
            src_ref=low_ref,
            dst_ref=from_next_ref,
            send_sem=low_send_sem,
            recv_sem=low_recv_sem,
            device_id=place(jnp.maximum(me - 1, 0)),
            device_id_type=MESH,
        )

    def high_copy():
        return pltpu.make_async_remote_copy(
            src_ref=high_ref,
            dst_ref=from_prev_ref,
            send_sem=high_send_sem,
            recv_sem=high_recv_sem,
            device_id=place(jnp.minimum(me + 1, devices - 1)),
            device_id_type=MESH,
        )

    @pl.when(me > 0)
    def _():
        low_copy().start()

    high_ref[...] = packed(tile_sums(2 * patches))

    @pl.when(me < devices - 1)
    def _():
        high_copy().start()

    tiles_ref[...] = tile_sums(patches)
    row = iota(square, 0)
    in_order = (column == row % 8 * (LANES // 8) + row // 8).astype(jnp.float32)
    in_order = in_order.astype(jnp.bfloat16)
    for block in range(blocks):
        at = slice(LANES * block, LANES * (block + 1))
        ordered = jnp.dot(in_order, focus_ref[at, :], preferred_element_type=jnp.float32)
        focused_ref[at, :] = jnp.dot(
            ordered.astype(jnp.bfloat16), parts_beside, preferred_element_type=jnp.float32
        ).astype(jnp.bfloat16)
    others = pl.ds(0, devices - 1)
    pltpu.make_async_copy(send_ref.at[others], send_ref.at[others], send_sem).wait()

    @pl.when(me < devices - 1)
    def _():
        low_copy().wait_recv()
        tiles_ref[...] += unpacked(from_next_ref)

    @pl.when(me > 0)
    def _():
        high_copy().wait_recv()
        tiles_ref[...] += unpacked(from_prev_ref)

    @pl.when(me > 0)
    def _():
        low_copy().wait_send()

    @pl.when(me < devices - 1)
    def _():
        high_copy().wait_send()


def hand_out(focused_ref, tiles_ref, focused_out, tiles_out, sems):
    copies = (
        pltpu.make_async_copy(focused_ref, focused_out, sems.at[0]),
        pltpu.make_async_copy(tiles_ref, tiles_out, sems.at[1]),
    )
    for copy in copies:
        copy.start()
    for copy in copies:
        copy.wait()


def body(
    raw_echoes, range_taps, mig_offset, interp_band, interp_table, azimuth_taps, geo_list, geo_frac
):
    across = lax.axis_size("range")
    devices = lax.axis_size("pulse") * across
    rows, breadth = raw_echoes.shape
    pulses = rows * devices
    bins = breadth // 2
    chunks = bins // LANES
    patches = geo_list.shape[1]
    tile = PROWS * (bins // devices)
    rwidth = min(bins, range_taps.shape[0] + LANES)
    awidth = min(pulses, azimuth_taps.shape[0] + LANES)
    spare = 0 if chunks == GROUP else rwidth // LANES
    whole = pl.BlockSpec(memory_space=pltpu.VMEM)
    operands = (
        raw_echoes,
        range_taps.T,
        mig_offset.reshape(1, bins),
        interp_band.reshape(1, bins),
        interp_table.T,
        azimuth_taps.T,
        geo_list[0].T,
        geo_frac[0].T,
    )
    scratch = [pltpu.VMEM(operand.shape, operand.dtype) for operand in operands] + [
        pltpu.VMEM((LANES, rwidth), jnp.bfloat16),
        pltpu.VMEM((LANES, rwidth), jnp.bfloat16),
        pltpu.VMEM((LANES, rwidth), jnp.bfloat16),
        pltpu.VMEM((2 * LANES, awidth), jnp.bfloat16),
        pltpu.VMEM(((chunks + spare) * rows, 2 * LANES), jnp.bfloat16),
        pltpu.VMEM((GROUP * rows, 2 * LANES), jnp.float32),
        pltpu.VMEM(((chunks + 2) * rows, 2 * LANES), jnp.bfloat16),
        pltpu.VMEM((interp_table.shape[1], bins), jnp.float32),
        pltpu.VMEM((chunks, 2 * LANES, LANES), jnp.bfloat16),
        pltpu.VMEM((devices, rows, LANES), jnp.bfloat16),
        pltpu.VMEM((devices, rows, LANES), jnp.bfloat16),
        pltpu.VMEM((pulses, LANES), jnp.bfloat16),
        pltpu.VMEM((pulses // LANES, 2 * LANES, LANES), jnp.float32),
        pltpu.VMEM((pulses // 8, LANES), jnp.float32),
        pltpu.VMEM((2 * patches, tile // 2), jnp.bfloat16),
        pltpu.VMEM((2 * patches, tile // 2), jnp.bfloat16),
        pltpu.VMEM((2 * patches, tile // 2), jnp.bfloat16),
        pltpu.VMEM((2 * patches, tile // 2), jnp.bfloat16),
    ] + [
        pltpu.SemaphoreType.DMA((8,)),
        pltpu.SemaphoreType.DMA,
        pltpu.SemaphoreType.DMA((pulses // LANES,)),
    ] + [pltpu.SemaphoreType.DMA] * 4
    shapes = (
        jax.ShapeDtypeStruct((pulses, breadth // devices), jnp.bfloat16),
        jax.ShapeDtypeStruct((patches, tile), jnp.float32),
    )
    outside = pl.BlockSpec(memory_space=pltpu.HBM)
    results = pl.pallas_call(
        functools.partial(kernel, devices, across),
        out_shape=shapes,
        in_specs=[outside] * 8,
        out_specs=(whole, whole),
        scratch_shapes=scratch,
        compiler_params=pltpu.CompilerParams(
            collective_id=0, has_side_effects=True, vmem_limit_bytes=40 * 2**20
        ),
    )(*[pltpu.with_memory_space_constraint(operand, pltpu.HBM) for operand in operands])
    return pl.pallas_call(
        hand_out,
        out_shape=shapes,
        in_specs=[whole] * 2,
        out_specs=(outside, outside),
        scratch_shapes=[pltpu.SemaphoreType.DMA((2,))],
    )(*[pltpu.with_memory_space_constraint(result, pltpu.VMEM) for result in results])


def solution(mesh):
    placed = (
        P(("pulse", "range"), None),
        P(),
        P(),
        P(),
        P(),
        P(),
        P(("pulse", "range"), None, None),
        P(("pulse", "range"), None, None),
    )
    return jax.shard_map(
        body,
        mesh=mesh,
        in_specs=placed,
        out_specs=(P(None, ("pulse", "range")), P(("pulse", "range"), None)),
        check_vma=False,
    )
```
